32 devices in a mesh: width: 4 (over y, core), dp: 8 (over z, x).
Axes of the slice: x: 2, y: 2, z: 4, core: 2. Of those that a mesh axis runs over, the one named last changes fastest.
Arguments:
- inputs: bfloat16 [4, 8192, 768], P('width', 'dp'), may hold values from -6 to 6
- cotangent: bfloat16 [4, 8192, 768], P('width', 'dp'), may hold values from -6 to 6
- replacement_ids: int32 [4, 8192], P('width', 'dp'), may hold values from 0 to 1023
- augmented_count: int32 [4, 8], P('width', 'dp'), may hold values from 0 to 1024
- segment_ids: int32 [4, 8, 1024], P('width', 'dp'), may hold values from 0 to 3, never falling along the last dimension, each value on 1 to 512 neighbouring positions
- query_weight: bfloat16 [768, 768], P('dp'), may hold values from -0.21875 to 0.21875
- key_weight: bfloat16 [768, 768], P('dp'), may hold values from -0.21875 to 0.21875
- value_weight: bfloat16 [768, 768], P('dp'), may hold values from -0.21875 to 0.21875
- output_weight: bfloat16 [768, 768], P('dp'), may hold values from -2.5 to 2.5
- inner_weight: bfloat16 [768, 3072], P('dp'), may hold values from -0.21875 to 0.21875
- outer_weight: bfloat16 [3072, 768], P('dp'), may hold values from -0.15625 to 0.15625
- query_bias: bfloat16 [768], P('dp'), may hold values from -3 to 3
- value_bias: bfloat16 [768], P('dp'), may hold values from -3 to 3
- output_bias: bfloat16 [768], P('dp'), may hold values from -3 to 3
- inner_bias: bfloat16 [3072], P('dp'), may hold values from -3 to 3
- outer_bias: bfloat16 [768], P('dp'), may hold values from -3 to 3
- attention_gain: bfloat16 [768], P('dp'), may hold values from 0.25 to 1.75
- attention_shift: bfloat16 [768], P('dp'), may hold values from -3 to 3
- feed_gain: bfloat16 [768], P('dp'), may hold values from 0.25 to 1.75
- feed_shift: bfloat16 [768], P('dp'), may hold values from -3 to 3
Outputs:
- block_output: bfloat16 [4, 8192, 768], P('width', 'dp')
- input_gradient: float32 [4, 8192, 768], P('width', 'dp')
- grad_query_weight: float32 [768, 768], P('dp')
- grad_key_weight: float32 [768, 768], P('dp')
- grad_value_weight: float32 [768, 768], P('dp')
- grad_output_weight: float32 [768, 768], P('dp')
- grad_inner_weight: float32 [768, 3072], P('dp')
- grad_outer_weight: float32 [3072, 768], P('dp')
- grad_query_bias: float32 [768], P('dp')
- grad_value_bias: float32 [768], P('dp')
- grad_output_bias: float32 [768], P('dp')
- grad_inner_bias: float32 [3072], P('dp')
- grad_outer_bias: float32 [768], P('dp')
- grad_attention_gain: float32 [768], P('dp')
- grad_attention_shift: float32 [768], P('dp')
- grad_feed_gain: float32 [768], P('dp')
- grad_feed_shift: float32 [768], P('dp')
The draws below stay inside these ranges and needn't reach their ends.
Inputs may be any that keep to these rules, and one draw needn't show every extreme that they name: `replacement_ids`: a position within the token's own sequence. `segment_ids`: never falling along a sequence; each document spans 1 to 512 positions.
All inputs are finite; a program needn't handle non-finite values.
Results may differ from the reference program's by a relative error of at most 0.013.
The reference program's roundings to bfloat16 on the way count: a program that leaves them out, or rounds other values in their place, can miss the bound.
Values may be sent and summed in bfloat16 or wider, within the bound.
No kernel may reach another device: no remote copies, remote signals or barrier semaphores. Data moves between devices by JAX's collectives and lax.ppermute only.
A program may use at most 256 MiB of HBM per device.

```python
import math
import jax
import jax.numpy as jnp
import numpy as np
from jax import lax

D = 768
HEADS = 12
HEAD_DIM = 64
FF = 3072
SEQ_LEN = 1024
DOCS = 4
GROUPS = 4
TOKENS = 8192
N_DP = 8


def touch_ends(entries, key, smallest, high):
    spot = [jax.random.randint(jax.random.fold_in(key, axis), (), 0, length) for axis, length in enumerate(entries.shape)]
    widest = entries.shape.index(max(entries.shape))
    neighbour = spot[:widest] + [(spot[widest] + 1) % entries.shape[widest]] + spot[widest + 1:]
    return entries.at[tuple(spot)].set(smallest).at[tuple(neighbour)].set(high)


def raised(drawn, stream_key, source, target, blocks, factor):
    def block_of(position):
        return (jnp.arange(drawn.shape[position]) // (drawn.shape[position] // blocks)).reshape((-1,) + (1,) * (drawn.ndim - 1 - position))

    first = jax.random.permutation(stream_key, blocks)[block_of(target)]
    far = (block_of(target) + blocks // 2) % blocks
    return jnp.where((block_of(source) == first) | (block_of(source) == far), factor * drawn, drawn)


def block_scale(key, shape, shards, least, largest):
    factor_of, own = 1.0, jax.random.fold_in(key, 6)
    for position, shards_of in shards:
        draws = jnp.exp(jax.random.uniform(jax.random.fold_in(own, position), (shards_of,), jnp.float32, least / len(shards), largest / len(shards)))
        factor_of = factor_of * jnp.repeat(draws, shape[position] // shards_of).reshape([-1 if axis == position else 1 for axis in range(len(shape))])
    return factor_of


def split_up(number_of, total, bound, slope):
    weights = [(1 << 20) // math.isqrt(grade ** slope) + 1 for grade in range(2, number_of + 1)]
    rest, holding = total - bound - (number_of - 1), [1] * (number_of - 1)
    while rest > 0:
        movable = [i for i in range(number_of - 1) if holding[i] < bound]
        mass, remaining = sum([weights[i] for i in movable]), rest
        for i in movable:
            extra = min(bound - holding[i], max(1, remaining * weights[i] // mass), rest)
            holding[i] = holding[i] + extra
            rest = rest - extra
    return np.array([bound] + holding)


def uneven_parts(key, count, total, most, lean):
    if count == 2:
        one = jax.random.randint(key, (), max(1, total - most), min(most, total - 1) + 1)
        return jnp.stack([one, total - one])
    sizes = jnp.asarray(split_up(count, total, most, lean), jnp.int32)
    twos = (count - 1) // 2
    source_of, sink = sizes[1:1 + 2 * twos:2], sizes[2:2 + 2 * twos:2]
    room = jnp.minimum(source_of - 1, most - sink)
    moved = jax.random.randint(jax.random.fold_in(key, 1), (twos,), 0, 1 << 20) % (room + 1)
    sizes = sizes.at[1:1 + 2 * twos:2].set(source_of - moved).at[2:2 + 2 * twos:2].set(sink + moved)
    return sizes[jax.random.permutation(jax.random.fold_in(key, 2), count)]


def scatter_about(rng, dims, width, reach, cuts=(), kind=jnp.bfloat16):
    entries = jax.random.normal(rng, dims, jnp.float32) * width
    if len(cuts) > 0:
        entries = block_scale(rng, dims, cuts, -0.22, 0.18) * entries
    return jnp.clip(entries, min=-reach, max=reach).astype(kind)


def bell_draw_with(own_key, dims, scale, most, shards, heavy, kind=jnp.bfloat16):
    values = scale * jax.random.normal(own_key, dims, jnp.float32)
    if shards:
        values = values * block_scale(own_key, dims, shards, -0.22, 0.18)
    return jnp.clip(raised(values, jax.random.fold_in(own_key, 3), *heavy), -most, most).astype(kind)


def setup_inputs(seed: int = 0) -> dict:
    arg_keys = jax.random.split(jax.random.key(seed), 21)
    return {
        "inputs": bell_draw_with(arg_keys[0], (GROUPS, TOKENS, D), 1.0, 6.0, ((0, 4), (1, 8)), (1, 2, 8, 2.0)),
        "cotangent": scatter_about(arg_keys[1], (GROUPS, TOKENS, D), 1.0, 6.0, ((0, 4), (1, 8))),
        "replacement_ids": touch_ends(jax.random.randint(arg_keys[2], (GROUPS, TOKENS), 0, SEQ_LEN), jax.random.fold_in(arg_keys[2], 1), 0, SEQ_LEN - 1).astype(jnp.int32),
        "augmented_count": touch_ends(jax.random.randint(arg_keys[3], (GROUPS, N_DP), 0, SEQ_LEN + 1), jax.random.fold_in(arg_keys[3], 1), 0, SEQ_LEN).astype(jnp.int32),
        "segment_ids": jax.vmap(lambda own: jnp.searchsorted(jnp.cumsum(uneven_parts(own, DOCS, SEQ_LEN, SEQ_LEN // 2, 1)), jnp.arange(SEQ_LEN), side="right"))(jax.random.split(arg_keys[4], GROUPS * N_DP)).reshape((GROUPS, N_DP, SEQ_LEN)).astype(jnp.int32),
        "query_weight": scatter_about(arg_keys[5], (D, D), D ** -0.5, 0.21875, ((0, 8),)),
        "key_weight": scatter_about(arg_keys[6], (D, D), D ** -0.5, 0.21875, ((0, 8),)),
        "value_weight": scatter_about(arg_keys[7], (D, D), D ** -0.5, 0.21875, ((0, 8),)),
        "output_weight": scatter_about(arg_keys[8], (D, D), (max(1, D * 8 // SEQ_LEN)) ** -0.5, 2.5, ((0, 8),)),
        "inner_weight": scatter_about(arg_keys[9], (D, FF), D ** -0.5, 0.21875, ((0, 8),)),
        "outer_weight": scatter_about(arg_keys[10], (FF, D), (FF // 2) ** -0.5, 0.15625, ((0, 8),)),
        "query_bias": scatter_about(arg_keys[11], (D,), 0.5, 3.0, ((0, 8),)),
        "value_bias": scatter_about(arg_keys[12], (D,), 0.5, 3.0, ((0, 8),)),
        "output_bias": scatter_about(arg_keys[13], (D,), 0.5, 3.0, ((0, 8),)),
        "inner_bias": scatter_about(arg_keys[14], (FF,), 0.5, 3.0, ((0, 8),)),
        "outer_bias": scatter_about(arg_keys[15], (D,), 0.5, 3.0, ((0, 8),)),
        "attention_gain": jnp.clip(1.0 + 0.15 * jax.random.normal(arg_keys[16], (D,), jnp.float32), 0.25, 1.75).astype(jnp.bfloat16),
        "attention_shift": scatter_about(arg_keys[17], (D,), 0.5, 3.0, ((0, 8),)),
        "feed_gain": jnp.clip(1.0 + 0.15 * jax.random.normal(arg_keys[18], (D,), jnp.float32), 0.25, 1.75).astype(jnp.bfloat16),
        "feed_shift": scatter_about(arg_keys[19], (D,), 0.5, 3.0, ((0, 8),)),
    }


EPSILON = 1e-12
NEGATIVE = -1000000000.0
PRECISE = lax.Precision.HIGHEST

@jax.custom_vjp
def low(v):
    return lax.optimization_barrier(v.astype(jnp.bfloat16)).astype(jnp.float32)

@jax.custom_vjp
def low_back(v):
    return v

def low_keep(v):
    return (low(v), None)

def low_pass(kept, grad):
    return (grad,)

def back_keep(v):
    return (v, None)

def back_low(kept, grad):
    return (low(grad),)
low.defvjp(low_keep, low_pass)
low_back.defvjp(back_keep, back_low)

def layer_norm(hidden, scaling, offset):
    average = lax.optimization_barrier(jnp.mean(hidden, axis=-1, keepdims=True))
    centred = hidden - average
    variance = lax.optimization_barrier(jnp.mean(centred * centred, axis=-1, keepdims=True))
    return centred * lax.rsqrt(variance + EPSILON) * scaling + offset

def gelu_exact(values):
    return jax.nn.gelu(values, approximate=False)

def sequence_forward(weights, heads_used, units_used, sequence, replaced, augmented, segment_row):
    query_weight, key_weight, value_weight, output_weight, inner_weight, outer_weight, query_bias, value_bias, output_bias, inner_bias, outer_bias, attention_gain, attention_shift, feed_gain, feed_shift = weights
    width_used = heads_used * HEAD_DIM
    positions = jnp.arange(SEQ_LEN, dtype=jnp.int32)
    sources = jnp.where(positions < augmented, replaced, positions).astype(jnp.int32)
    mixed_rows = jnp.take(sequence, sources, axis=0)
    mixed_low = low(mixed_rows)
    queries = low(low_back(jnp.dot(mixed_low, query_weight[:, :width_used], precision=PRECISE) + query_bias[:width_used]))
    key_heads = low(low_back(jnp.dot(mixed_low, key_weight[:, :width_used], precision=PRECISE)))
    values = low(low_back(jnp.dot(mixed_low, value_weight[:, :width_used], precision=PRECISE) + value_bias[:width_used]))
    query_split = queries.reshape(SEQ_LEN, heads_used, HEAD_DIM)
    key_split = key_heads.reshape(SEQ_LEN, heads_used, HEAD_DIM)
    value_split = values.reshape(SEQ_LEN, heads_used, HEAD_DIM)
    scores = low_back(jnp.einsum('qhd,khd->hqk', query_split, key_split, precision=PRECISE) * HEAD_DIM ** (-0.5))
    allowed = segment_row[:, None] == segment_row[None, :]
    scores = jnp.where(allowed[None], scores, NEGATIVE)
    probability = low(jax.nn.softmax(scores, axis=-1))
    context = jnp.einsum('hqk,khd->qhd', probability, value_split, precision=PRECISE).reshape(SEQ_LEN, width_used)
    context = low(low_back(context))
    attention = low_back(jnp.dot(context, output_weight[:width_used], precision=PRECISE) + output_bias)
    normed = layer_norm(mixed_rows + attention, attention_gain, attention_shift)
    normed_low = low(normed)
    inner_value = low_back(jnp.dot(normed_low, inner_weight[:, :units_used], precision=PRECISE) + inner_bias[:units_used])
    activated = low(gelu_exact(inner_value))
    outer_value = low_back(jnp.dot(activated, outer_weight[:units_used], precision=PRECISE) + outer_bias)
    return layer_norm(normed + outer_value, feed_gain, feed_shift)

def group_forward(weights, group_inputs, replaced, augmented, group_segments, heads_used, units_used):

    def single(weight_set, sequence, replaced_row, augmented_one, segment_row):
        return sequence_forward(weight_set, heads_used, units_used, sequence, replaced_row, augmented_one, segment_row)
    checked = jax.checkpoint(single)

    def scanner(carried, pieces):
        return (carried, checked(weights, pieces[0], pieces[1], pieces[2], pieces[3]))
    _, outputs = lax.scan(scanner, jnp.zeros((), jnp.float32), (group_inputs, replaced, augmented, group_segments))
    return outputs

def reference(inputs, cotangent, replacement_ids, augmented_count, segment_ids, query_weight, key_weight, value_weight, output_weight, inner_weight, outer_weight, query_bias, value_bias, output_bias, inner_bias, outer_bias, attention_gain, attention_shift, feed_gain, feed_shift):
    weights = tuple((entry.astype(jnp.float32) for entry in (query_weight, key_weight, value_weight, output_weight, inner_weight, outer_weight, query_bias, value_bias, output_bias, inner_bias, outer_bias, attention_gain, attention_shift, feed_gain, feed_shift)))
    totals = tuple((jnp.zeros_like(entry) for entry in weights))
    outputs = []
    input_grads = []
    for width_index in range(GROUPS):
        heads_used = HEADS * (width_index + 1) // GROUPS
        units_used = FF * (width_index + 1) // GROUPS
        group_inputs = inputs[width_index].astype(jnp.float32).reshape(N_DP, SEQ_LEN, D)
        replaced = replacement_ids[width_index].reshape(N_DP, SEQ_LEN).astype(jnp.int32)
        augmented = augmented_count[width_index].astype(jnp.int32)
        group_segments = segment_ids[width_index]

        def forward(weight_set, sequences):
            return group_forward(weight_set, sequences, replaced, augmented, group_segments, heads_used, units_used)
        result, backward = jax.vjp(forward, weights, group_inputs)
        weight_grads, sequence_grads = backward(cotangent[width_index].astype(jnp.float32).reshape(N_DP, SEQ_LEN, D))
        totals = tuple((first + second for first, second in zip(totals, weight_grads)))
        outputs.append(result.reshape(TOKENS, D).astype(jnp.bfloat16))
        input_grads.append(sequence_grads.reshape(TOKENS, D))
    return (jnp.stack(outputs), jnp.stack(input_grads), totals[0], totals[1], totals[2], totals[3], totals[4], totals[5], totals[6], totals[7], totals[8], totals[9], totals[10], totals[11], totals[12], totals[13], totals[14])
```

```python
import functools

import jax
import jax.numpy as jnp
from jax import lax
from jax.experimental import pallas as pl
from jax.experimental.pallas import tpu as pltpu
from jax.sharding import PartitionSpec as P

HEADS = 12
HEAD_DIM = 64
EPSILON = 1e-12
NEGATIVE = -1000000000.0
QB = 256
PIECES = 8
WIDTHS = 4
bf16 = jnp.bfloat16
f32 = jnp.float32
MIB = 2**20
NN = (((1,), (0,)), ((), ()))
NT = (((1,), (1,)), ((), ()))
TN = (((0,), (0,)), ((), ()))
SMEM = pl.BlockSpec(memory_space=pltpu.SMEM)
ANY = pl.BlockSpec(memory_space=pl.ANY)


def dot(a, b, dims=NN):
    return lax.dot_general(a, b, dims, preferred_element_type=f32)


def params(mib):
    return pltpu.CompilerParams(vmem_limit_bytes=mib * MIB)


def cost(flops, moved, transcendentals=0):
    return pl.CostEstimate(flops=flops, bytes_accessed=moved, transcendentals=transcendentals)


def whole(shape):
    return pl.BlockSpec(shape, lambda *_: (0,) * len(shape))


def shape_of(shape, kind=bf16):
    return jax.ShapeDtypeStruct(shape, kind)


def slot_of(piece, home):
    return ((piece & 1) ^ (home & 1)) * 4 + ((piece >> 1) ^ (home >> 1))


def mix_kernel(src_ref, x_ref, mixed_ref):
    rows, total = src_ref.shape[0], x_ref.shape[0]
    pick = src_ref[...] == lax.broadcasted_iota(jnp.int32, (rows, total), 1)
    mixed_ref[...] = dot(jnp.where(pick, 1.0, 0.0).astype(bf16), x_ref[...]).astype(bf16)


def mix(src_col, x):
    total, width = x.shape
    return pl.pallas_call(
        mix_kernel,
        in_specs=[whole((total, 1)), whole((total, width))],
        out_specs=whole((total, width)),
        out_shape=shape_of((total, width)),
        compiler_params=params(24),
        cost_estimate=cost(2 * total * total * width, 4 * total * width),
        name="mix",
    )(src_col, x)


def fetch_halves(sc, sources, weights, sem):
    rows = weights.shape[1] // PIECES
    for other, source in enumerate(sources):
        half = (sc[0] & 1) ^ other
        for piece in range(PIECES):
            pltpu.make_async_copy(
                source.at[slot_of(piece, sc[1]), pl.ds(0, rows), :],
                weights.at[half, pl.ds(piece * rows, rows), :],
                sem,
            ).start()


def project_kernel(sc, mixed_ref, bias_ref, own, other, q_ref, k_ref, v_ref, weights, sem):
    part = weights.shape[2] // 3

    @pl.when(pl.program_id(0) == 0)
    def _():
        fetch_halves(sc, (own, other), weights, sem)
        pltpu.make_async_copy(weights, weights, sem).wait()

    for half in range(2):
        out = dot(mixed_ref[...], weights[half]) + bias_ref[half : half + 1, :].astype(f32)
        here = slice(half * part, (half + 1) * part)
        q_ref[:, here] = out[:, :part].astype(bf16) * jnp.asarray(HEAD_DIM**-0.5, bf16)
        k_ref[:, here] = out[:, part : 2 * part].astype(bf16)
        v_ref[:, here] = out[:, 2 * part :].astype(bf16)


def project(sc, mixed, bias, own, other, tile=512):
    total, width = mixed.shape
    columns = own.shape[2]
    rows = pl.BlockSpec((tile, width), lambda i: (i, 0))
    return pl.pallas_call(
        project_kernel,
        grid=(total // tile,),
        in_specs=[SMEM, rows, whole(bias.shape), ANY, ANY],
        out_specs=[rows] * 3,
        out_shape=[shape_of((total, width))] * 3,
        scratch_shapes=[pltpu.VMEM((2, width, columns), bf16), pltpu.SemaphoreType.DMA],
        compiler_params=params(40),
        cost_estimate=cost(4 * total * width * columns, 12 * total * width),
        name="project",
    )(sc, mixed, bias, own, other)


def keep_lanes(value, head):
    lane = lax.broadcasted_iota(jnp.int32, value.shape, 1)
    return jnp.where(lane // HEAD_DIM == head, value, jnp.zeros_like(value))


def for_window(windows, block, total, run):
    start = pl.multiple_of(windows[0, block], 128)
    need = windows[1, block]
    for size in range(QB, total + 1, QB):

        @pl.when(need == size)
        def _():
            run(start, size)


def attend_kernel(sc, windows, seg_col, seg_row, q_ref, k_ref, v_ref, ctx_ref, lse_ref, vt_ref):
    total = q_ref.shape[0]
    left = sc[3] - 2 * pl.program_id(0)

    @pl.when(left <= 0)
    def _():
        ctx_ref[...] = jnp.zeros_like(ctx_ref)
        lse_ref[...] = jnp.zeros_like(lse_ref)

    @pl.when(left > 0)
    def _():
        vt_ref[...] = v_ref[...].T
        for block in range(total // QB):

            def run(start, size, block=block):
                here = pl.ds(block * QB, QB)
                keys = k_ref[pl.ds(start, size), :]
                queries = q_ref[here, :]
                allowed = seg_col[pl.ds(start, size), :] == seg_row[:, here]
                parts = []
                for head in range(2):
                    s = dot(keys, keep_lanes(queries, head), NT)
                    s = jnp.where(allowed, s, NEGATIVE)
                    top = jnp.max(s, axis=0, keepdims=True)
                    e = jnp.exp(s - top)
                    norm = jnp.sum(e, axis=0, keepdims=True)
                    values = vt_ref[head * HEAD_DIM : (head + 1) * HEAD_DIM, pl.ds(start, size)]
                    parts.append(dot(values, e.astype(bf16)) * (1.0 / norm))
                    lse_ref[0, head : head + 1, here] = top + jnp.log(norm)
                both = jnp.concatenate(parts, axis=0).T
                lane = lax.broadcasted_iota(jnp.int32, both.shape, 1)
                ctx_ref[here, :] = jnp.where(lane < left * HEAD_DIM, both, 0.0).astype(bf16)

            for_window(windows, block, total, run)


def attend(sc, windows, seg_col, seg_row, q, k, v):
    total, width = q.shape
    pairs = width // 128
    cols = pl.BlockSpec((total, 128), lambda i: (0, i))
    return pl.pallas_call(
        attend_kernel,
        grid=(pairs,),
        in_specs=[SMEM, SMEM, whole(seg_col.shape), whole(seg_row.shape), cols, cols, cols],
        out_specs=[cols, pl.BlockSpec((1, 2, total), lambda i: (i, 0, 0))],
        out_shape=[shape_of((total, width)), shape_of((pairs, 2, total), f32)],
        scratch_shapes=[pltpu.VMEM((128, total), bf16)],
        compiler_params=params(40),
        cost_estimate=cost(16 * total * total * width, 8 * total * width, total * total * HEADS),
        name="attend",
    )(sc, windows, seg_col, seg_row, q, k, v)


def attend_back_kernel(
    first, sc, windows, seg_col, seg_row, q_ref, k_ref, v_ref, c_ref, lse_ref,
    dq_ref, dk_ref, dv_ref, kt_ref, dk_sum, dv_sum,
):
    total = q_ref.shape[0]
    left = sc[3] - 2 * (pl.program_id(0) + first)

    @pl.when(left <= 0)
    def _():
        for ref in (dq_ref, dk_ref, dv_ref):
            ref[...] = jnp.zeros_like(ref)

    @pl.when(left > 0)
    def _():
        kt_ref[...] = k_ref[...].T
        dk_sum[...] = jnp.zeros_like(dk_sum)
        dv_sum[...] = jnp.zeros_like(dv_sum)
        for block in range(total // QB):

            def run(start, size, block=block):
                here = pl.ds(block * QB, QB)
                there = pl.ds(start, size)
                keys = k_ref[there, :]
                values = v_ref[there, :]
                allowed = seg_col[there, :] == seg_row[:, here]
                qs = [keep_lanes(q_ref[here, :], head) for head in range(2)]
                cs = [keep_lanes(c_ref[here, :], head) for head in range(2)]
                dq, weights, scores = [], [], []
                for head in range(2):
                    s = dot(keys, qs[head], NT)
                    dp = dot(values, cs[head], NT)
                    p = jnp.where(allowed, jnp.exp(s - lse_ref[0, head : head + 1, here]), 0.0)
                    t = p * dp
                    ds = (t - p * jnp.sum(t, axis=0, keepdims=True)).astype(bf16)
                    weights.append(p.astype(bf16))
                    scores.append(ds)
                    dq.append(dot(kt_ref[head * HEAD_DIM : (head + 1) * HEAD_DIM, there], ds))
                dv_sum[there, :] += dot(weights[0], cs[0]) + dot(weights[1], cs[1])
                dk_sum[there, :] += dot(scores[0], qs[0]) + dot(scores[1], qs[1])
                both = jnp.concatenate(dq, axis=0).T
                dq_ref[here, :] = (both * HEAD_DIM**-0.5).astype(bf16)

            for_window(windows, block, total, run)
        dk_ref[...] = dk_sum[...].astype(bf16)
        dv_ref[...] = dv_sum[...].astype(bf16)


def attend_back(half, sc, windows, seg_col, seg_row, q, k, v, c, lse):
    total, width = q.shape
    pairs = width // 256
    first = half * pairs
    cols = pl.BlockSpec((total, 128), lambda i: (0, i + first))
    return pl.pallas_call(
        functools.partial(attend_back_kernel, first),
        grid=(pairs,),
        in_specs=[SMEM, SMEM, whole(seg_col.shape), whole(seg_row.shape), cols, cols, cols, cols,
                  pl.BlockSpec((1, 2, total), lambda i: (i + first, 0, 0))],
        out_specs=[pl.BlockSpec((total, 128), lambda i: (0, i))] * 3,
        out_shape=[shape_of((total, width // 2))] * 3,
        scratch_shapes=[
            pltpu.VMEM((128, total), bf16),
            pltpu.VMEM((total, 128), f32),
            pltpu.VMEM((total, 128), f32),
        ],
        compiler_params=params(48),
        cost_estimate=cost(20 * total * total * width, 8 * total * width, total * total * HEADS // 2),
        name="attend_back",
    )(sc, windows, seg_col, seg_row, q, k, v, c, lse)


def row_mean(value):
    return jnp.mean(value, axis=1, keepdims=True)


def normalise(hidden):
    centred = hidden - row_mean(hidden)
    rate = lax.rsqrt(row_mean(centred * centred) + EPSILON)
    return centred * rate, rate


def norm_back(grad, gain, unit, rate):
    scaled = grad * gain
    return rate * (scaled - row_mean(scaled) - unit * row_mean(scaled * unit))


def col_sum(value):
    return jnp.sum(value, axis=0, keepdims=True)


def feed_kernel(
    sc, mixed_ref, ctx_ref, cot_ref, bi_ref, vec_ref, f0, f1, f2, f3,
    out_ref, first_ref, dctx_ref, dwo_ref, dbi_ref, sums_ref, keep_i, send_i, keep_u, send_u,
    wi, wu, wo, act, slope, unit_ref, grad_ref, low_ref, glow_ref, rate_ref, stage,
    wo_sem, wi_sem, wu_sem, out_sem,
):
    total, width = mixed_ref.shape
    unit_rows = width // PIECES
    outer_rows = wi.shape[0] * width // PIECES
    own, home, active, heads = sc[0], sc[1], sc[2], sc[3]
    sources = (f0, f1, f2, f3)
    ob, g1, s1, ub, g2, s2 = (vec_ref[i : i + 1, :].astype(f32) for i in range(6))

    half_rows = unit_rows // 2
    for slot in range(2):
        for piece in range(PIECES):
            at = pl.multiple_of(piece * unit_rows + ((own & 1) ^ slot) * half_rows, 16)
            pltpu.make_async_copy(
                sources[slot].at[slot_of(piece, home), pl.ds(2 * unit_rows, half_rows), :],
                wo.at[pl.ds(at, half_rows), :],
                wo_sem,
            ).start()
    for slot in range(WIDTHS):
        for piece in range(PIECES):
            pltpu.make_async_copy(
                sources[slot].at[slot_of(piece, home), pl.ds(0, unit_rows), :],
                wi.at[slot, pl.ds(piece * unit_rows, unit_rows), :],
                wi_sem.at[slot],
            ).start()
        for end in range(2):
            for part in range(WIDTHS):
                at = pl.multiple_of(end * outer_rows + (own ^ part) * unit_rows, 16)
                pltpu.make_async_copy(
                    sources[part].at[slot_of(2 * (own ^ slot) + end, home), pl.ds(unit_rows, unit_rows), :],
                    wu.at[slot, pl.ds(at, unit_rows), :],
                    wu_sem.at[slot],
                ).start()

    step = 256
    blocks = [pl.ds(i * step, step) for i in range(total // step)]
    pltpu.make_async_copy(wo, wo, wo_sem).wait()
    for rows in blocks:
        unit, rate = normalise(mixed_ref[rows, :].astype(f32) + dot(ctx_ref[rows, :], wo[...]) + ob)
        unit_ref[rows, :] = unit
        rate_ref[rows, :] = rate
        normed = unit * g1 + s1
        low_ref[rows, :] = normed.astype(bf16)
        first_ref[rows, :] = normed + ub
    for slot in range(WIDTHS):
        quarter = own ^ slot
        pltpu.make_async_copy(wi.at[slot], wi.at[slot], wi_sem.at[slot]).wait()
        pltpu.make_async_copy(wu.at[slot], wu.at[slot], wu_sem.at[slot]).wait()

        @pl.when(quarter < active)
        def _():
            bias = bi_ref[quarter].astype(f32)
            for rows in blocks:
                inner = dot(low_ref[rows, :], wi[slot]) + bias
                phi = 0.5 * (1.0 + lax.erf(inner * 0.7071067811865476))
                act[slot, rows, :] = (inner * phi).astype(bf16)
                density = jnp.exp(-0.5 * inner * inner) * 0.3989422804014327
                slope[slot, rows, :] = (phi + inner * density).astype(bf16)
            first_ref[...] += dot(act[slot], wu[slot])

    sums_ref[...] = jnp.zeros_like(sums_ref)
    for rows in blocks:
        unit, rate = normalise(first_ref[rows, :])
        out_ref[rows, :] = (unit * g2 + s2).astype(bf16)
        cot = cot_ref[rows, :].astype(f32)
        grad = norm_back(cot, g2, unit, rate)
        grad_ref[rows, :] = grad
        low = grad.astype(bf16)
        glow_ref[rows, :] = low
        sums_ref[3:4, :] += col_sum(low.astype(f32))
        sums_ref[4:5, :] += col_sum(cot * unit)
        sums_ref[5:6, :] += col_sum(cot)
    first_ref[...] = grad_ref[...]

    for slot in range(WIDTHS):
        quarter = own ^ slot

        if slot > 0:
            for _ in range(2):
                pltpu.make_async_copy(stage.at[0], stage.at[0], out_sem).wait()

        @pl.when(quarter >= active)
        def _():
            stage[...] = jnp.zeros_like(stage)
            dbi_ref[quarter] = jnp.zeros((1, width), f32)

        @pl.when(quarter < active)
        def _():
            stage[1] = dot(act[slot], glow_ref[...], TN).astype(bf16)
            inner = (dot(glow_ref[...], wu[slot], NT) * slope[slot].astype(f32)).astype(bf16)
            dbi_ref[quarter] = col_sum(inner.astype(f32))
            stage[0] = dot(low_ref[...], inner, TN).astype(bf16)
            first_ref[...] += dot(inner, wi[slot], NT)

        to = (keep_i, send_i)[slot & 1]
        for piece in range(PIECES):
            pltpu.make_async_copy(
                stage.at[0, pl.ds(piece * unit_rows, unit_rows), :],
                to.at[slot >> 1, slot_of(piece, home)],
                out_sem,
            ).start()
        for end in range(2):
            for part in range(WIDTHS):
                at = pl.multiple_of(end * outer_rows + (own ^ part) * unit_rows, 16)
                pltpu.make_async_copy(
                    stage.at[1, pl.ds(at, unit_rows), :],
                    (keep_u, send_u)[part & 1].at[part >> 1, slot_of(2 * quarter + end, home)],
                    out_sem,
                ).start()

    for rows in blocks:
        unit = unit_ref[rows, :]
        normed_grad = first_ref[rows, :]
        first = norm_back(normed_grad, g1, unit, rate_ref[rows, :])
        first_ref[rows, :] = first
        low = first.astype(bf16)
        glow_ref[rows, :] = low
        dctx = dot(low, wo[...], NT)
        lane = lax.broadcasted_iota(jnp.int32, dctx.shape, 1)
        dctx_ref[rows, :] = jnp.where(lane < heads * HEAD_DIM, dctx, 0.0).astype(bf16)
        sums_ref[0:1, :] += col_sum(low.astype(f32))
        sums_ref[1:2, :] += col_sum(normed_grad * unit)
        sums_ref[2:3, :] += col_sum(normed_grad)
    dwo_ref[...] = dot(ctx_ref[...], glow_ref[...], TN).astype(bf16)
    for _ in range(2):
        pltpu.make_async_copy(stage.at[0], stage.at[0], out_sem).wait()


def feed(sc, mixed, ctx, cot, bi, vec, sources):
    total, width = mixed.shape
    square = whole((total, width))
    piece = (2, PIECES, width // PIECES, width)
    units = WIDTHS * width
    return pl.pallas_call(
        feed_kernel,
        in_specs=[SMEM, square, square, square, whole(bi.shape), whole(vec.shape)] + [ANY] * 4,
        out_specs=[square, square, square, whole((width, width)), whole((WIDTHS, 1, width)), whole((8, width))]
        + [ANY] * 4,
        out_shape=[
            shape_of((total, width)), shape_of((total, width), f32), shape_of((total, width)),
            shape_of((width, width)), shape_of((WIDTHS, 1, width), f32), shape_of((8, width), f32),
        ] + [shape_of(piece)] * 4,
        scratch_shapes=[
            pltpu.VMEM((WIDTHS, width, width), bf16), pltpu.VMEM((WIDTHS, width, width), bf16),
            pltpu.VMEM((width, width), bf16),
            pltpu.VMEM((WIDTHS, total, width), bf16), pltpu.VMEM((WIDTHS, total, width), bf16),
            pltpu.VMEM((total, width), f32), pltpu.VMEM((total, width), f32),
            pltpu.VMEM((total, width), bf16), pltpu.VMEM((total, width), bf16), pltpu.VMEM((total, 1), f32),
            pltpu.VMEM((2, width, width), bf16),
            pltpu.SemaphoreType.DMA, pltpu.SemaphoreType.DMA((WIDTHS,)), pltpu.SemaphoreType.DMA((WIDTHS,)),
            pltpu.SemaphoreType.DMA,
        ],
        compiler_params=params(60),
        cost_estimate=cost(2 * total * width * (6 * units + 3 * width), 40 * width * width, total * units),
        name="feed",
    )(sc, mixed, ctx, cot, bi, vec, *sources)


def project_grad_kernel(with_output, sc, mixed_ref, dq, dk, dv, *refs):
    dwo_ref = refs[0] if with_output else None
    keep, send, sums_ref = refs[-3:]
    width = mixed_ref.shape[1]
    part = dq.shape[1]
    rows = width // PIECES
    own, home = sc[0] & 1, sc[1]
    sums_ref[...] = jnp.zeros_like(sums_ref)

    def put(value, lanes, piece_of=lambda p: p):
        for piece in range(PIECES):
            slot = slot_of(piece, home)
            low = value[piece * rows : piece * rows + rows // 2]
            high = value[piece * rows + rows // 2 : (piece + 1) * rows]

            @pl.when(own == 0)
            def _():
                keep[slot, : rows // 2, lanes] = low
                send[slot, : rows // 2, lanes] = high

            @pl.when(own == 1)
            def _():
                keep[slot, : rows // 2, lanes] = high
                send[slot, : rows // 2, lanes] = low

    mixed = mixed_ref[...]
    for i, ref in enumerate((dq, dk, dv)):
        put(dot(mixed, ref[...], TN).astype(bf16), slice(i * part, (i + 1) * part))
        sums_ref[i : i + 1, :] = col_sum(ref[...].astype(f32))
    if with_output:
        put(dwo_ref[...], slice(3 * part, 3 * part + width))


def project_grad(sc, mixed, grads, dwo=None):
    total, width = mixed.shape
    part = grads[0].shape[1]
    rows = width // PIECES // 2
    columns = 3 * part + (0 if dwo is None else width)
    extra = [] if dwo is None else [dwo]
    pack = (PIECES, rows, columns)
    return pl.pallas_call(
        functools.partial(project_grad_kernel, dwo is not None),
        in_specs=[SMEM, whole((total, width))] + [whole((total, part))] * 3 + [whole(a.shape) for a in extra],
        out_specs=[whole(pack), whole(pack), whole((8, part))],
        out_shape=[shape_of(pack), shape_of(pack), shape_of((8, part), f32)],
        compiler_params=params(40),
        cost_estimate=cost(6 * total * width * part, 4 * total * width),
        name="project_grad",
    )(sc, mixed, *grads, *extra)


def input_grad_kernel(
    sc, src_row, first_ref, q0, k0, v0, q1, k1, v1, own, other, out_ref, weights, grads, hi_ref, lo_ref, sem
):
    total, width = first_ref.shape
    block = pl.program_id(0)
    rows = out_ref.shape[0]
    part = q0.shape[1]

    @pl.when(block == 0)
    def _():
        fetch_halves(sc, (own, other), weights, sem)
        for half, refs in enumerate(((q0, k0, v0), (q1, k1, v1))):
            for i, ref in enumerate(refs):
                grads[half, :, i * part : (i + 1) * part] = ref[...]
        pltpu.make_async_copy(weights, weights, sem).wait()
        grad = first_ref[...] + dot(grads[0], weights[0], NT) + dot(grads[1], weights[1], NT)
        hi = grad.astype(bf16)
        hi_ref[...] = hi
        lo_ref[...] = (grad - hi.astype(f32)).astype(bf16)

    target = lax.broadcasted_iota(jnp.int32, (rows, total), 0) + block * rows
    place = jnp.where(target == src_row[...], 1.0, 0.0).astype(bf16)
    out_ref[...] = dot(place, hi_ref[...]) + dot(place, lo_ref[...])


def input_grad(sc, src_row, first, halves, own, other, tile=512):
    total, width = first.shape
    part = halves[0][0].shape[1]
    columns = own.shape[2]
    return pl.pallas_call(
        input_grad_kernel,
        grid=(total // tile,),
        in_specs=[SMEM, whole(src_row.shape), whole((total, width))] + [whole((total, part))] * 6 + [ANY, ANY],
        out_specs=pl.BlockSpec((tile, width), lambda i: (i, 0)),
        out_shape=shape_of((total, width), f32),
        scratch_shapes=[
            pltpu.VMEM((2, width, columns), bf16), pltpu.VMEM((2, total, columns), bf16),
            pltpu.VMEM((total, width), bf16), pltpu.VMEM((total, width), bf16),
            pltpu.SemaphoreType.DMA,
        ],
        compiler_params=params(52),
        cost_estimate=cost(4 * total * width * columns + 4 * total * total * width, 20 * total * width),
        name="input_grad",
    )(sc, src_row, first, *halves[0], *halves[1], own, other)


def finish_kernel(
    sc, feed0, feed1, feed2, feed3, low_own, low_other, high_own, high_other,
    gq, gk, gv, go, gi, gu, *vectors,
):
    own = sc[0]
    rows, width = gq.shape
    half, part = rows // 2, width // 2
    for slot, ref in enumerate((feed0, feed1, feed2, feed3)):
        quarter = own ^ slot
        at = pl.multiple_of(quarter * width, 128)
        gi[:, pl.ds(at, width)] = ref[0].astype(f32)
        to = pl.multiple_of(quarter * rows, 8)
        gu[pl.ds(to, rows), :] = ref[1].astype(f32)
    for other, (low, high) in enumerate(((low_own, high_own), (low_other, high_other))):
        to = pl.ds(pl.multiple_of(((own & 1) ^ other) * half, 8), half)
        for i, ref in enumerate((gq, gk, gv)):
            ref[to, :part] = low[:half, i * part : (i + 1) * part].astype(f32)
            ref[to, part:] = high[:half, i * part : (i + 1) * part].astype(f32)
        go[to, :] = low[:half, 3 * part :].astype(f32)
    line = jnp.where(
        (own & 1) == 0, high_own[half : half + 16, :].astype(f32), high_other[half : half + 16, :].astype(f32)
    )
    at = 0
    for ref in vectors:
        size = ref.shape[1]
        ref[...] = line[0:1, at : at + size]
        at += size


def finish(sc, feeds, lows, highs, rows, width):
    sizes = [rows] * 8 + [WIDTHS * rows]
    shapes = [(rows, width)] * 4 + [(rows, WIDTHS * width), (WIDTHS * rows, width)] + [(1, n) for n in sizes]
    inputs = [*feeds, *lows, *highs]
    return pl.pallas_call(
        finish_kernel,
        in_specs=[SMEM] + [whole(a.shape) for a in inputs],
        out_specs=[whole(s) for s in shapes],
        out_shape=[shape_of(s, f32) for s in shapes],
        compiler_params=params(24),
        cost_estimate=cost(rows * width, 60 * rows * width),
        name="finish",
    )(sc, *inputs)


def exchange(value, axis, bits):
    size = lax.axis_size(axis)
    return lax.ppermute(value, axis, [(i, i ^ bits) for i in range(size)])


def gather_pieces(piece):
    column = jnp.stack([piece] + [exchange(piece, "dp", 2 * k) for k in (1, 2, 3)])
    return column, exchange(column, "dp", 1)


def add(*terms):
    total = terms[0].astype(f32)
    for term in terms[1:]:
        total = total + term.astype(f32)
    return total.astype(bf16)


def scatter_dp(value, axis=0):
    kept = lax.slice_in_dim(value, 0, 4, axis=axis)
    sent = lax.slice_in_dim(value, 4, 8, axis=axis)
    total = add(kept, exchange(sent, "dp", 1))
    pick = lambda k: lax.index_in_dim(total, k, axis=axis, keepdims=False)
    return add(pick(0), *[exchange(pick(k), "dp", 2 * k) for k in (1, 2, 3)])


def per_device(
    inputs, cotangent, replacement_ids, augmented_count, segment_ids,
    query_weight, key_weight, value_weight, output_weight, inner_weight, outer_weight,
    query_bias, value_bias, output_bias, inner_bias, outer_bias,
    attention_gain, attention_shift, feed_gain, feed_shift,
):
    total, width = inputs.shape[1:]
    group = lax.axis_index("width")
    groups = lax.axis_size("width")
    shards = lax.axis_size("dp")
    direct = shards == PIECES and groups == WIDTHS
    rows = query_weight.shape[0]
    part = width // 2
    heads = HEADS * (group + 1) // groups
    place = lax.axis_index("dp")
    own, home = (group, place) if direct else (jnp.zeros_like(group), jnp.zeros_like(place))
    sc = jnp.stack([own, home, group + 1, heads]).astype(jnp.int32)

    positions = jnp.arange(total, dtype=jnp.int32)
    sources = jnp.where(positions < augmented_count[0, 0], replacement_ids[0], positions)
    segments = segment_ids[0, 0]
    seg_col, seg_row = segments[:, None], segments[None, :]
    windows = window_table(segments)
    mixed = mix(sources[:, None], inputs[0])

    vectors = (query_bias, value_bias, output_bias, attention_gain, attention_shift,
               outer_bias, feed_gain, feed_shift, inner_bias)
    if direct:
        line = jnp.concatenate(vectors)[None]
        start = (group & 1) * part
        cut = [lax.dynamic_slice_in_dim(a, start, part, 1) for a in (query_weight, key_weight, value_weight)]
        pack = jnp.concatenate([jnp.concatenate(cut, 1), line, jnp.zeros((15, 3 * part), bf16)])
        near, far = gather_pieces(pack)
        qkv_own = jnp.concatenate([near, far])
        qkv_other = exchange(qkv_own, "width", 1)
        feed_pack = jnp.concatenate([
            lax.dynamic_slice_in_dim(inner_weight, group * width, width, 1),
            lax.dynamic_slice_in_dim(outer_weight, group * rows, rows, 0),
            lax.dynamic_slice_in_dim(output_weight, (group & 1) * (rows // 2), rows // 2, 0),
        ])
        near, far = gather_pieces(feed_pack)
        feed0 = jnp.concatenate([near, far])
        feed2 = exchange(feed0, "width", 2)
        feed1 = exchange(feed0, "width", 1)
        feed3 = exchange(feed2, "width", 1)
        order = jnp.stack([slot_of(p, home) for p in range(PIECES)])
        lines = jnp.take(qkv_own[:, rows, :], order, axis=0)
    else:
        everything = lambda a: lax.all_gather(a, "dp", axis=0, tiled=True)
        slots = [(s & 3) * 2 + (s >> 2) for s in range(PIECES)]
        by_piece = lambda a: jnp.stack([a.reshape(PIECES, -1, a.shape[-1])[p] for p in slots])
        full = [everything(a) for a in (query_weight, key_weight, value_weight)]
        qkv_own, qkv_other = (
            by_piece(jnp.concatenate([a[:, h * part : (h + 1) * part] for a in full], 1)) for h in range(2)
        )
        piece_rows = width // PIECES
        inner_full, outer_full, output_full = (
            everything(a) for a in (inner_weight, outer_weight, output_weight)
        )
        outer_parts = by_piece(outer_full).reshape(PIECES, WIDTHS, piece_rows, width)
        output_parts = by_piece(output_full).reshape(PIECES, 2, piece_rows // 2, width)
        feed0, feed1, feed2, feed3 = (
            jnp.concatenate([
                by_piece(inner_full[:, q * width : (q + 1) * width]),
                outer_parts[:, q],
                output_parts[:, q & 1],
            ], 1)
            for q in range(WIDTHS)
        )
        lines = jnp.concatenate([everything(a).reshape(PIECES, -1) for a in vectors], 1)
    small = lines[:, :width].reshape(PIECES, 8, width // PIECES).transpose(1, 0, 2).reshape(8, width)
    inner_bias_full = lines[:, width:].reshape(WIDTHS, 1, width)
    none = jnp.zeros((part,), bf16)
    qkv_bias = jnp.stack([
        jnp.concatenate([small[0, h * part : (h + 1) * part], none, small[1, h * part : (h + 1) * part]])
        for h in range(2)
    ])
    vec = small[2:]

    q, k, v = project(sc, mixed, qkv_bias, qkv_own, qkv_other)
    ctx, lse = attend(sc, windows, seg_col, seg_row, q, k, v)
    out, first, dctx, dwo, dbi, sums, keep_i, send_i, keep_u, send_u = feed(
        sc, mixed, ctx, cotangent[0], inner_bias_full, vec, (feed0, feed1, feed2, feed3)
    )
    low = attend_back(0, sc, windows, seg_col, seg_row, q, k, v, dctx, lse)
    keep_low, send_low, sums_low = project_grad(sc, mixed, low, dwo)
    high = attend_back(1, sc, windows, seg_col, seg_row, q, k, v, dctx, lse)
    keep_high, send_high, sums_high = project_grad(sc, mixed, high)
    input_gradient = input_grad(sc, sources[None, :], first, (low, high), qkv_own, qkv_other)

    vector_grads = [
        jnp.concatenate([sums_low[0], sums_high[0]]), jnp.concatenate([sums_low[2], sums_high[2]]),
        sums[0], sums[1], sums[2], sums[3], sums[4], sums[5],
    ]
    grad_lines = jnp.concatenate(
        [jnp.stack(vector_grads).reshape(8, PIECES, -1).transpose(1, 0, 2).reshape(PIECES, width),
         dbi.reshape(PIECES, -1)], 1)
    if direct:
        part_i = add(keep_i, exchange(send_i, "width", 1))
        part_u = add(keep_u, exchange(send_u, "width", 1))
        part_i = add(part_i[0], exchange(part_i[1], "width", 2))
        part_u = scatter_dp(part_u, axis=1)
        part_i = scatter_dp(part_i)
        part_u = add(part_u[0], exchange(part_u[1], "width", 2))
        feed_sum0 = jnp.stack([part_i, part_u])
        feed_sum2 = exchange(feed_sum0, "width", 2)
        feed_sum1 = exchange(feed_sum0, "width", 1)
        feed_sum3 = exchange(feed_sum2, "width", 1)
        low_sum = scatter_dp(add(keep_low, exchange(send_low, "width", 1)))
        low_sum = add(low_sum, exchange(low_sum, "width", 2))
        low_other = exchange(low_sum, "width", 1)
        lines_slot = jnp.take(grad_lines, jnp.stack([((s & 3) ^ (home >> 1)) * 2 + ((s >> 2) ^ (home & 1)) for s in range(PIECES)]), axis=0)
        lines_slot = jnp.pad(lines_slot.astype(bf16)[:, None], ((0, 0), (0, 15), (0, 0)))
        blank = jnp.zeros_like(lines_slot)
        even = (group & 1) == 0
        keep_high = jnp.concatenate([keep_high, jnp.where(even, lines_slot, blank)], 1)
        send_high = jnp.concatenate([send_high, jnp.where(even, blank, lines_slot)], 1)
        high_sum = scatter_dp(add(keep_high, exchange(send_high, "width", 1)))
        high_sum = add(high_sum, exchange(high_sum, "width", 2))
        high_other = exchange(high_sum, "width", 1)
        results = finish(
            sc, (feed_sum0, feed_sum1, feed_sum2, feed_sum3), (low_sum, low_other), (high_sum, high_other),
            rows, width)
        matrices, lines_out = results[:6], [a[0] for a in results[6:]]
        (gq, gk, gv, go, gi, gu) = matrices
        (bq, bv, bo, ga, sa, bu, gf, sf, bi) = lines_out
    else:
        ordered = [(p & 1) * 4 + (p >> 1) for p in range(PIECES)]
        back = lambda a: jnp.stack([a[s] for s in ordered])
        total_sum = lambda a: lax.psum(lax.psum_scatter(a.astype(f32), "dp", scatter_dimension=0, tiled=True), "width")
        quarters_i = [keep_i[0], send_i[0], keep_i[1], send_i[1]]
        quarters_u = [keep_u[0], send_u[0], keep_u[1], send_u[1]]
        gi = total_sum(jnp.concatenate([back(a).reshape(width, width) for a in quarters_i], 1))
        gu = total_sum(jnp.stack([back(a) for a in quarters_u], 1).reshape(-1, width))
        low_full = jnp.concatenate([back(keep_low), back(send_low)], 1).reshape(width, -1)
        high_full = jnp.concatenate([back(keep_high), back(send_high)], 1).reshape(width, -1)
        gq, gk, gv = (
            total_sum(jnp.concatenate([a[:, i * part : (i + 1) * part] for a in (low_full, high_full)], 1))
            for i in range(3)
        )
        go = total_sum(low_full[:, 3 * part :])
        bq, bv, bo, ga, sa, bu, gf, sf = (total_sum(a) for a in vector_grads)
        bi = total_sum(dbi.reshape(-1))
    return (out[None], input_gradient[None], gq, gk, gv, go, gi, gu, bq, bv, bo, bi, bu, ga, sa, gf, sf)


def window_table(segments):
    total = segments.shape[0]
    blocks = segments.reshape(total // QB, QB)
    low = jnp.sum((segments[None, :] < blocks[:, :1]).astype(jnp.int32), axis=1)
    high = jnp.sum((segments[None, :] <= blocks[:, -1:]).astype(jnp.int32), axis=1)
    start = low // 128 * 128
    size = (high - start + QB - 1) // QB * QB
    return jnp.stack([jnp.minimum(start, total - size), size])


def solution(mesh):
    tokens = (P("width", "dp", None),) * 2 + (P("width", "dp"),) * 2 + (P("width", "dp", None),)
    matrices = (P("dp", None),) * 6
    vectors = (P("dp"),) * 9
    return jax.shard_map(
        per_device,
        mesh=mesh,
        in_specs=tokens + matrices + vectors,
        out_specs=(P("width", "dp", None),) * 2 + matrices + vectors,
        check_vma=False,
    )
```

```python
import functools

import jax
import jax.numpy as jnp
from jax import lax
from jax.experimental import pallas as pl
from jax.experimental.pallas import tpu as pltpu
from jax.sharding import PartitionSpec as P

HEADS = 12
HEAD_DIM = 64
EPSILON = 1e-12
NEGATIVE = -1000000000.0
DOCS = 4
LONGEST = 512
BIG = float(2**30)
PIECES = 8
WIDTH = ("y", "core")
DP = ("z", "x")
WIDTHS = 4
bf16 = jnp.bfloat16
f32 = jnp.float32
MIB = 2**20
NN = (((1,), (0,)), ((), ()))
NT = (((1,), (1,)), ((), ()))
TN = (((0,), (0,)), ((), ()))
SMEM = pl.BlockSpec(memory_space=pltpu.SMEM)
ANY = pl.BlockSpec(memory_space=pl.ANY)


def dot(a, b, dims=NN):
    return lax.dot_general(a, b, dims, preferred_element_type=f32)


def params(mib):
    return pltpu.CompilerParams(vmem_limit_bytes=mib * MIB)


SHORT = pl.CostEstimate(flops=1, bytes_accessed=1, transcendentals=0)


def ignoring(kernel, at, count):
    return lambda *refs: kernel(*refs[:at], *refs[at + count :])


def whole(shape):
    return pl.BlockSpec(shape, lambda *_: (0,) * len(shape))


def shape_of(shape, kind=bf16):
    return jax.ShapeDtypeStruct(shape, kind)


def slot_of(piece, home):
    return ((piece & 1) ^ (home & 1)) * 4 + ((piece >> 1) ^ (home >> 1))


def mix_kernel(src_ref, x_ref, mixed_ref):
    rows, total = src_ref.shape[0], x_ref.shape[0]
    pick = src_ref[...] == lax.broadcasted_iota(jnp.int32, (rows, total), 1)
    mixed_ref[...] = dot(jnp.where(pick, 1.0, 0.0).astype(bf16), x_ref[...]).astype(bf16)


def mix(src_col, x):
    total, width = x.shape
    return pl.pallas_call(
        mix_kernel,
        in_specs=[whole((total, 1)), whole((total, width))],
        out_specs=whole((total, width)),
        out_shape=shape_of((total, width)),
        compiler_params=params(24),
        cost_estimate=SHORT,
        name="mix",
    )(src_col, x)


def pack_kernel(sc, wq, wv, near_ref):
    half, part = wq.shape[0] // 2, wq.shape[1] // 2
    rows = pl.ds(pl.multiple_of((sc[0] >> 1) * half, 16), half)
    lanes = pl.ds(pl.multiple_of((sc[0] & 1) * part, 128), part)
    near_ref[:half, :] = wv[rows, lanes]
    near_ref[half:, :] = wq[rows, lanes]


def pack(sc, wq, wv):
    rows, width = wq.shape
    shape = rows, width // 2
    return pl.pallas_call(
        pack_kernel,
        in_specs=[SMEM, whole(wq.shape), whole(wv.shape)],
        out_specs=whole(shape),
        out_shape=shape_of(shape),
        compiler_params=params(8),
        cost_estimate=SHORT,
        name="pack",
    )(sc, wq, wv)


def pack_key_kernel(sc, wk, *refs):
    vectors, key_ref = refs[:9], refs[-1]
    rows, part = wk.shape[0], wk.shape[1] // 2
    line = jnp.concatenate([ref[...].astype(f32) for ref in vectors], axis=1)
    lines = [line[:, i * part : (i + 1) * part] for i in range(3)] + [jnp.zeros((13, part), f32)]
    key_ref[:rows, :] = wk[:, pl.ds(pl.multiple_of((sc[0] & 1) * part, 128), part)]
    key_ref[rows:, :] = jnp.concatenate(lines, axis=0).astype(bf16)


def pack_key(sc, wk, vectors, dep):
    rows, width = wk.shape
    lines = [v[None] for v in vectors]
    shape = rows + 16, width // 2
    return pl.pallas_call(
        ignoring(pack_key_kernel, 2 + len(lines), 1),
        in_specs=[SMEM] + [whole(a.shape) for a in (wk, *lines)] + [ANY],
        out_specs=whole(shape),
        out_shape=shape_of(shape),
        compiler_params=params(8),
        cost_estimate=SHORT,
        name="pack_key",
    )(sc, wk, *lines, dep)


def pack_inner_kernel(sc, wi, inner_ref):
    width = inner_ref.shape[1]
    inner_ref[...] = wi[:, pl.ds(pl.multiple_of(sc[0] * width, 128), width)]


def pack_inner(sc, wi, dep):
    shape = wi.shape[0], wi.shape[1] // WIDTHS
    return pl.pallas_call(
        ignoring(pack_inner_kernel, 2, 1),
        in_specs=[SMEM, whole(wi.shape), ANY],
        out_specs=whole(shape),
        out_shape=shape_of(shape),
        compiler_params=params(8),
        cost_estimate=SHORT,
        name="pack_inner",
    )(sc, wi, dep)


def pack_rest_kernel(sc, wo, wu, rest_ref):
    rows = wo.shape[0]
    rest_ref[: 2 * rows, :] = wu[pl.ds(pl.multiple_of((sc[0] & 1) * 2 * rows, 16), 2 * rows), :]
    rest_ref[2 * rows :, :] = wo[pl.ds(pl.multiple_of((sc[0] & 1) * (rows // 2), 16), rows // 2), :]


def pack_rest(sc, wo, wu, dep):
    rows, width = wo.shape
    shape = rows * 5 // 2, width
    return pl.pallas_call(
        ignoring(pack_rest_kernel, 3, 1),
        in_specs=[SMEM, whole(wo.shape), whole(wu.shape), ANY],
        out_specs=whole(shape),
        out_shape=shape_of(shape),
        compiler_params=params(8),
        cost_estimate=SHORT,
        name="pack_rest",
    )(sc, wo, wu, dep)


def fetch_parts(sc, sources, base, weight, sem):
    rows, part = weight.shape[0] // PIECES, weight.shape[1] // 2
    step = rows // 2
    for slot, source in enumerate(sources):
        where = sc[0] ^ slot
        at = pl.multiple_of((where & 1) * part, 128)
        for piece in range(PIECES):
            to = pl.multiple_of(piece * rows + (where >> 1) * step, 16)
            pltpu.make_async_copy(
                source.at[slot_of(piece, sc[1]), pl.ds(base, step), :],
                weight.at[pl.ds(to, step), pl.ds(at, part)],
                sem,
            ).start()


def fetch_halves(sc, sources, weight, sem):
    rows, part = weight.shape[0] // PIECES, weight.shape[1] // 2
    for other, source in enumerate(sources):
        at = pl.multiple_of(((sc[0] & 1) ^ other) * part, 128)
        for piece in range(PIECES):
            pltpu.make_async_copy(
                source.at[slot_of(piece, sc[1]), pl.ds(0, rows), :],
                weight.at[pl.ds(piece * rows, rows), pl.ds(at, part)],
                sem,
            ).start()


def project_kernel(fetch, scale, sc, mixed_ref, bias_ref, *refs):
    parts, outs, (weight, sem) = refs[:-5], refs[-5:-2], refs[-2:]
    fetch(sc, parts, weight, sem)
    pltpu.make_async_copy(weight, weight, sem).wait()
    for start in range(0, mixed_ref.shape[0], 512):
        rows = pl.ds(start, 512)
        out = dot(mixed_ref[rows, :], weight[...]) + bias_ref[...].astype(f32)
        out = out.astype(bf16) * jnp.asarray(scale, bf16)
        for third, ref in enumerate(outs):
            size = ref.shape[1]
            ref[rows, :] = out[:, third * size : (third + 1) * size]


def project(base, scale, sc, mixed, bias, parts):
    total, width = mixed.shape
    fetch = fetch_halves if base is None else lambda sc, parts, weight, sem: fetch_parts(sc, parts, base, weight, sem)
    return pl.pallas_call(
        functools.partial(project_kernel, fetch, scale),
        in_specs=[SMEM, whole((total, width)), whole((1, width))] + [ANY] * len(parts),
        out_specs=[whole((total, width // 3))] * 3 + [whole((width, width))],
        out_shape=[shape_of((total, width // 3))] * 3 + [shape_of((width, width))],
        scratch_shapes=[pltpu.SemaphoreType.DMA],
        compiler_params=params(24),
        cost_estimate=SHORT,
        name="project",
    )(sc, mixed, bias, *parts)


def doc_table(segments):
    number = jnp.arange(DOCS)[:, None]
    return jnp.stack([
        jnp.sum((segments[None, :] < number).astype(jnp.int32), axis=1),
        jnp.sum((segments[None, :] == number).astype(jnp.int32), axis=1),
    ])


def head_rows(value):
    lane = lax.broadcasted_iota(jnp.int32, value.shape, 1)
    none = jnp.zeros_like(value)
    return jnp.concatenate(
        [jnp.where(lane < HEAD_DIM, value, none), jnp.where(lane < HEAD_DIM, none, value)], axis=0
    )


def over_docs(docs, sizes, run):
    @pl.loop(0, DOCS)
    def _(doc):
        start, length = docs[0, doc], docs[1, doc]
        low = 0
        for size in sizes:

            @pl.when((length > low) & (length <= size))
            def _():
                run(start, length, size)

            low = size


def mask_columns(length, queries, keys):
    lane = lax.broadcasted_iota(jnp.int32, (keys, 128), 1)
    row = lax.broadcasted_iota(jnp.int32, (keys, 128), 0)
    of_keys = jnp.where((lane == 0) & (row >= length), 1.0, 0.0).astype(bf16)
    lane = lax.broadcasted_iota(jnp.int32, (queries, 128), 1)
    return jnp.where(lane == 0, -BIG, 0.0).astype(bf16), of_keys


def unpack(pairs, total, moves):
    for pair in range(pairs):
        for source, to in moves:
            to[pair, :total, :] = source[:, 128 * pair : 128 * (pair + 1)].astype(f32)
            to[pair, total:, :] = jnp.zeros((LONGEST, 128), f32)


def attend_kernel(first, pairs, sc, docs, q_ref, k_ref, v_ref, ctx_ref, wide_ref, lse_ref, qs, ks, vs, cs, ls):
    total = q_ref.shape[0]
    left = sc[3] - 2 * first
    step = 256

    @pl.when(left <= 0)
    def _():
        for ref in (ctx_ref, wide_ref, lse_ref):
            ref[...] = jnp.zeros_like(ref)

    @pl.when(left > 0)
    def _():
        unpack(pairs, total, ((q_ref, qs), (k_ref, ks), (v_ref, vs)))
        lane = lax.broadcasted_iota(jnp.int32, (step, 128), 1)

        def run(start, length, size):
            @pl.loop(0, (length + step - 1) // step)
            def _(block):
                rows, keys = pl.ds(start + block * step, step), pl.ds(start, size)
                of_queries, of_keys = mask_columns(length, 2 * step, size)
                stat = jnp.zeros((step, 128), f32)
                for pair in range(pairs):
                    queries = jnp.concatenate([head_rows(qs[pair, rows, :].astype(bf16)), of_queries], axis=1)
                    s = dot(queries, jnp.concatenate([ks[pair, keys, :].astype(bf16), of_keys], axis=1), NT)
                    top = jnp.max(s, axis=1, keepdims=True)
                    e = jnp.exp(s - top).astype(bf16)
                    values = jnp.concatenate([vs[pair, keys, :].astype(bf16), jnp.ones((size, 128), bf16)], axis=1)
                    out = dot(e, values)
                    norm = out[:, 128:129]
                    out = out[:, :128] * (1.0 / norm)
                    cs[pair, rows, :] = jnp.where(lane < HEAD_DIM, out[:step], out[step:])
                    logsum = top + jnp.log(norm)
                    stat = jnp.where(
                        lane == 2 * pair, logsum[:step], jnp.where(lane == 2 * pair + 1, logsum[step:], stat)
                    )
                ls[rows, :] = stat

        over_docs(docs, (256, 512), run)
        lane = lax.broadcasted_iota(jnp.int32, (total, 128), 1)
        for pair in range(pairs):
            lanes = slice(128 * pair, 128 * (pair + 1))
            value = jnp.where(lane < (left - 2 * pair) * HEAD_DIM, cs[pair, :total, :], 0.0)
            wide_ref[:, lanes] = value
            ctx_ref[:, lanes] = value.astype(bf16)
        lse_ref[...] = ls[:total, :]


def attend(third, sc, docs, q, k, v, deps=()):
    total, width = q.shape
    pairs = width // 128
    cols = out = whole((total, width))
    return pl.pallas_call(
        ignoring(functools.partial(attend_kernel, pairs * third, pairs), 5, len(deps)),
        in_specs=[SMEM, SMEM, cols, cols, cols] + [ANY] * len(deps),
        out_specs=[out, out, whole((total, 128))],
        out_shape=[shape_of((total, width)), shape_of((total, width), f32), shape_of((total, 128), f32)],
        scratch_shapes=[pltpu.VMEM((pairs, total + LONGEST, 128), f32)] * 4 + [pltpu.VMEM((total + LONGEST, 128), f32)],
        compiler_params=params(32),
        cost_estimate=SHORT,
        name="attend",
    )(sc, docs, q, k, v, *deps)


def attend_back_kernel(
    first, pairs, sc, docs, q_ref, k_ref, v_ref, c_ref, wide_ref, lse_ref,
    dq_ref, dk_ref, dv_ref, sums_ref, qs, ks, vs, cs, xs, ls,
):
    total = q_ref.shape[0]
    left = sc[3] - 2 * first

    @pl.when(left <= 0)
    def _():
        for ref in (dq_ref, dk_ref, dv_ref, sums_ref):
            ref[...] = jnp.zeros_like(ref)

    @pl.when(left > 0)
    def _():
        unpack(pairs, total, ((q_ref, qs), (k_ref, ks), (v_ref, vs), (c_ref, cs), (wide_ref, xs)))
        ls[:total, :] = lse_ref[...]
        ls[total:, :] = jnp.zeros((LONGEST, 128), f32)

        def run(start, length, size):
            rows = pl.ds(start, size)
            lane = lax.broadcasted_iota(jnp.int32, (size, 128), 1)
            live = lax.broadcasted_iota(jnp.int32, (size, 128), 0) < length
            of_queries, of_keys = mask_columns(length, 2 * size, size)
            logsums = jnp.where(live, ls[rows, :], BIG)
            for pair in range(pairs):
                queries = head_rows(qs[pair, rows, :].astype(bf16))
                grad = jnp.where(live, cs[pair, rows, :], 0.0)
                grads = head_rows(grad.astype(bf16))
                inner = grad * xs[pair, rows, :]
                delta = jnp.concatenate([
                    jnp.sum(jnp.where(lane < HEAD_DIM, inner, 0.0), axis=1, keepdims=True),
                    jnp.sum(jnp.where(lane < HEAD_DIM, 0.0, inner), axis=1, keepdims=True),
                ], axis=0)
                logsum = jnp.concatenate(
                    [logsums[:, 2 * pair : 2 * pair + 1], logsums[:, 2 * pair + 1 : 2 * pair + 2]], axis=0
                )
                keys = ks[pair, rows, :].astype(bf16)
                s = dot(jnp.concatenate([queries, of_queries], axis=1), jnp.concatenate([keys, of_keys], axis=1), NT)
                dp = dot(grads, vs[pair, rows, :].astype(bf16), NT)
                p = jnp.exp(s - logsum)
                ds = (p * (dp - delta)).astype(bf16)
                dv = dot(p.astype(bf16), grads, TN)
                dk = dot(ds, queries, TN)
                dq = dot(ds, keys)
                dq = jnp.where(lane < HEAD_DIM, dq[:size], dq[size:]) * HEAD_DIM**-0.5
                qs[pair, rows, :] = jnp.where(live, dq, qs[pair, rows, :])
                ks[pair, rows, :] = jnp.where(live, dk, ks[pair, rows, :])
                vs[pair, rows, :] = jnp.where(live, dv, vs[pair, rows, :])

        over_docs(docs, (128, 256, 384, 512), run)
        for pair in range(pairs):
            lanes = slice(128 * pair, 128 * (pair + 1))
            for to, value in ((dq_ref, qs), (dk_ref, ks), (dv_ref, vs)):
                to[:, lanes] = value[pair, :total, :].astype(bf16)
        sums_ref[0:1, :] = col_sum(dq_ref[...].astype(f32))
        sums_ref[1:2, :] = col_sum(dv_ref[...].astype(f32))


def attend_back(third, sc, docs, q, k, v, c, wide, lse, deps=()):
    total, width = q.shape
    pairs = width // 128
    cols = out = whole((total, width))
    return pl.pallas_call(
        ignoring(functools.partial(attend_back_kernel, pairs * third, pairs), 8, len(deps)),
        in_specs=[SMEM, SMEM, cols, cols, cols, cols, out, whole((total, 128))] + [ANY] * len(deps),
        out_specs=[out] * 3 + [whole((8, width))],
        out_shape=[shape_of((total, width))] * 3 + [shape_of((8, width), f32)],
        scratch_shapes=[pltpu.VMEM((pairs, total + LONGEST, 128), f32)] * 5 + [pltpu.VMEM((total + LONGEST, 128), f32)],
        compiler_params=params(40),
        cost_estimate=SHORT,
        name="attend_back",
    )(sc, docs, q, k, v, c, wide, lse, *deps)


def row_mean(value):
    return jnp.mean(value, axis=1, keepdims=True)


def normalise(hidden):
    centred = hidden - row_mean(hidden)
    rate = lax.rsqrt(row_mean(centred * centred) + EPSILON)
    return centred * rate, rate


def norm_back(grad, gain, unit, rate):
    scaled = grad * gain
    return rate * (scaled - row_mean(scaled) - unit * row_mean(scaled * unit))


def col_sum(value):
    return jnp.sum(value, axis=0, keepdims=True)


def feed_kernel(
    sc, mixed_ref, c0, c1, c2, cot_hbm, bi_ref, vec_ref, *refs
):
    inner_parts, rest = refs[:4], refs[4]
    (out_hbm, first_ref, d0, d1, d2, flow_ref, dbi_ref, sums_ref, keep_i, send_i, keep_u, send_u,
     wi, wu, wo, act, slope, unit_ref, grad_ref, low_ref, glow_ref, rate_ref, cot_ref, stage,
     wo_sem, wi_sem, wu_sem, stage_sem, cot_sem, out_sem) = refs[5:]
    total, width = mixed_ref.shape
    unit_rows = width // PIECES
    outer_rows = WIDTHS * width // PIECES
    own, home, active, heads = sc[0], sc[1], sc[2], sc[3]
    ob, g1, s1, ub, g2, s2 = (vec_ref[i : i + 1, :].astype(f32) for i in range(6))

    for half in range(2):
        pltpu.make_async_copy(
            rest.at[half, :, pl.ds(2 * unit_rows, unit_rows // 2), :], wo.at[:, half], wo_sem.at[half]
        ).start()
    for slot in range(WIDTHS):
        pltpu.make_async_copy(inner_parts[slot], wi.at[slot], wi_sem.at[slot]).start()
        for half in range(2):
            pltpu.make_async_copy(
                rest.at[half, pl.ds(2 * (own ^ slot), 2), pl.ds(0, 2 * unit_rows), :],
                wu.at[slot, :, half],
                wu_sem.at[slot, half],
            ).start()
    cot_copy = pltpu.make_async_copy(cot_hbm, cot_ref, cot_sem)
    cot_copy.start()

    def outer(slot):
        return wu[slot].reshape(width, width)

    def output():
        return wo[...].reshape(width, width)

    step = 256
    blocks = [pl.ds(i * step, step) for i in range(total // step)]
    for half in range(2):
        pltpu.make_async_copy(wo.at[:, half], wo.at[:, half], wo_sem.at[half]).wait()
    for rows in blocks:
        ctx = jnp.concatenate([c0[rows, :], c1[rows, :], c2[rows, :]], axis=1)
        unit, rate = normalise(mixed_ref[rows, :].astype(f32) + dot(ctx, output()) + ob)
        unit_ref[rows, :] = unit
        rate_ref[rows, :] = rate
        normed = unit * g1 + s1
        low_ref[rows, :] = normed.astype(bf16)
        first_ref[rows, :] = normed + ub
    for slot in range(WIDTHS):
        quarter = own ^ slot
        pltpu.make_async_copy(wi.at[slot], wi.at[slot], wi_sem.at[slot]).wait()
        for half in range(2):
            pltpu.make_async_copy(wu.at[slot, :, half], wu.at[slot, :, half], wu_sem.at[slot, half]).wait()

        @pl.when(quarter < active)
        def _():
            bias = bi_ref[quarter].astype(f32)
            for rows in blocks:
                inner = dot(low_ref[rows, :], wi[slot]) + bias
                phi = 0.5 * (1.0 + lax.erf(inner * 0.7071067811865476))
                act[slot, rows, :] = (inner * phi).astype(bf16)
                density = jnp.exp(-0.5 * inner * inner) * 0.3989422804014327
                slope[slot, rows, :] = (phi + inner * density).astype(bf16)
            first_ref[...] += dot(act[slot], outer(slot))

    sums_ref[...] = jnp.zeros_like(sums_ref)
    cot_copy.wait()
    for rows in blocks:
        unit, rate = normalise(first_ref[rows, :])
        cot = cot_ref[rows, :].astype(f32)
        cot_ref[rows, :] = (unit * g2 + s2).astype(bf16)
        grad = norm_back(cot, g2, unit, rate)
        grad_ref[rows, :] = grad
        low = grad.astype(bf16)
        glow_ref[rows, :] = low
        sums_ref[3:4, :] += col_sum(low.astype(f32))
        sums_ref[4:5, :] += col_sum(cot * unit)
        sums_ref[5:6, :] += col_sum(cot)
    out_copy = pltpu.make_async_copy(cot_ref, out_hbm, out_sem)
    out_copy.start()
    first_ref[...] = grad_ref[...]

    def staged(slot):
        for i in range(2):
            pltpu.make_async_copy(stage.at[slot & 1, i], stage.at[slot & 1, i], stage_sem.at[slot & 1, i]).wait()

    for slot in range(WIDTHS):
        quarter = own ^ slot
        here = slot & 1

        if slot > 1:
            staged(slot)

        @pl.when(quarter >= active)
        def _():
            stage[here] = jnp.zeros((2, width, width), bf16)
            dbi_ref[quarter] = jnp.zeros((1, width), f32)

        @pl.when(quarter < active)
        def _():
            stage[here, 1] = dot(act[slot], glow_ref[...], TN).astype(bf16)
            inner = (dot(glow_ref[...], outer(slot), NT) * slope[slot].astype(f32)).astype(bf16)
            dbi_ref[quarter] = col_sum(inner.astype(f32))
            stage[here, 0] = dot(low_ref[...], inner, TN).astype(bf16)
            first_ref[...] += dot(inner, wi[slot], NT)

        to = (keep_i, send_i)[slot & 1]
        for piece in range(PIECES):
            pltpu.make_async_copy(
                stage.at[here, 0, pl.ds(piece * unit_rows, unit_rows), :],
                to.at[slot >> 1, slot_of(piece, home)],
                stage_sem.at[here, 0],
            ).start()
        for end in range(2):
            for part in range(WIDTHS):
                at = pl.multiple_of(end * outer_rows + (own ^ part) * unit_rows, 16)
                pltpu.make_async_copy(
                    stage.at[here, 1, pl.ds(at, unit_rows), :],
                    (keep_u, send_u)[part & 1].at[part >> 1, slot_of(2 * quarter + end, home)],
                    stage_sem.at[here, 1],
                ).start()

    for rows in blocks:
        unit = unit_ref[rows, :]
        normed_grad = first_ref[rows, :]
        first = norm_back(normed_grad, g1, unit, rate_ref[rows, :])
        first_ref[rows, :] = first
        low = first.astype(bf16)
        flow_ref[rows, :] = low
        dctx = dot(low, output(), NT)
        lane = lax.broadcasted_iota(jnp.int32, dctx.shape, 1)
        dctx = jnp.where(lane < heads * HEAD_DIM, dctx, 0.0).astype(bf16)
        for third, ref in enumerate((d0, d1, d2)):
            size = ref.shape[1]
            ref[rows, :] = dctx[:, third * size : (third + 1) * size]
        sums_ref[0:1, :] += col_sum(low.astype(f32))
        sums_ref[1:2, :] += col_sum(normed_grad * unit)
        sums_ref[2:3, :] += col_sum(normed_grad)
    staged(WIDTHS - 2)
    staged(WIDTHS - 1)
    out_copy.wait()


def feed(sc, mixed, contexts, cot, bi, vec, inner_parts, rest):
    total, width = mixed.shape
    square = whole((total, width))
    piece = (2, PIECES, width // PIECES, width)
    return pl.pallas_call(
        feed_kernel,
        in_specs=[SMEM, square] + [whole((total, width // 3))] * 3 + [ANY, whole(bi.shape), whole(vec.shape)]
        + [ANY] * 5,
        out_specs=[ANY, square] + [whole((total, width // 3))] * 3 + [square, whole((WIDTHS, 1, width)), whole((8, width))]
        + [ANY] * 4,
        out_shape=[
            shape_of((total, width)), shape_of((total, width), f32), *[shape_of((total, width // 3))] * 3,
            shape_of((total, width)), shape_of((WIDTHS, 1, width), f32), shape_of((8, width), f32),
        ] + [shape_of(piece)] * 4,
        scratch_shapes=[
            pltpu.VMEM((WIDTHS, width, width), bf16), pltpu.VMEM((WIDTHS, 2, 2, width // 4, width), bf16),
            pltpu.VMEM((PIECES, 2, width // PIECES // 2, width), bf16),
            pltpu.VMEM((WIDTHS, total, width), bf16), pltpu.VMEM((WIDTHS, total, width), bf16),
            pltpu.VMEM((total, width), f32), pltpu.VMEM((total, width), f32),
            pltpu.VMEM((total, width), bf16), pltpu.VMEM((total, width), bf16), pltpu.VMEM((total, 1), f32),
            pltpu.VMEM((total, width), bf16), pltpu.VMEM((2, 2, width, width), bf16),
            pltpu.SemaphoreType.DMA((2,)), pltpu.SemaphoreType.DMA((WIDTHS,)), pltpu.SemaphoreType.DMA((WIDTHS, 2)),
            pltpu.SemaphoreType.DMA((2, 2)), pltpu.SemaphoreType.DMA, pltpu.SemaphoreType.DMA,
        ],
        compiler_params=params(60),
        cost_estimate=SHORT,
        name="feed",
    )(sc, mixed, *contexts, cot, bi, vec, *[a.reshape(width, width) for a in inner_parts], rest)


def project_grad_kernel(thirds, with_lines, plain, sc, mixed_ref, ctx0, ctx1, ctx2, low_ref, *refs):
    grads, lines = refs[: 3 * len(thirds)], refs[3 * len(thirds)] if with_lines else None
    keep, send = refs[-2:]
    total, width = mixed_ref.shape
    part = width // 3
    rows = width // PIECES
    own, home = sc[0], sc[1]
    for matrix in range(4):
        if matrix < 3:
            left = mixed_ref[...]
            right = jnp.concatenate([grads[3 * i + matrix][...] for i in range(len(thirds))], axis=1)
        else:
            left = jnp.concatenate([ctx0[...], ctx1[...], ctx2[...]], axis=1)
            right = low_ref[:, thirds[0] * part : (thirds[-1] + 1) * part]
        value = dot(left, right, TN).astype(bf16)
        slot = matrix ^ own

        def put(ref):
            for piece in range(PIECES):
                side, to = (matrix >> 1, piece) if plain else (slot >> 1, slot_of(piece, home))
                ref[side, to, pl.ds(0, rows), :] = value[piece * rows : (piece + 1) * rows]
                if with_lines:
                    ref[side, to, pl.ds(rows, 16), :] = lines[piece, matrix]

        @pl.when((slot & 1) == 0)
        def _():
            put(keep)

        @pl.when((slot & 1) == 1)
        def _():
            put(send)


def project_grad(thirds, sc, mixed, contexts, low, grads, lines=None, deps=(), plain=False):
    total, width = mixed.shape
    part = width // 3
    extra = [] if lines is None else [lines]
    flat = [a for group in grads for a in group]
    pack = (2, PIECES, width // PIECES + 16 * len(extra), part * len(thirds))
    count = 6 + len(flat) + len(extra)
    return pl.pallas_call(
        ignoring(functools.partial(project_grad_kernel, thirds, bool(extra), plain), count, len(deps)),
        in_specs=[SMEM, whole((total, width))] + [whole((total, part))] * 3 + [whole((total, width))]
        + [whole((total, part))] * len(flat) + [whole(a.shape) for a in extra] + [ANY] * len(deps),
        out_specs=[whole(pack), whole(pack)],
        out_shape=[shape_of(pack), shape_of(pack)],
        compiler_params=params(32),
        cost_estimate=SHORT,
        name="project_grad",
    )(sc, mixed, *contexts, low, *flat, *extra, *deps)


def input_grad_kernel(src_row, first_ref, wq, wk, wv, *refs):
    grads, out_ref, joined, hi_ref, lo_ref = refs[:-4], *refs[-4:]
    total, width = first_ref.shape
    block = pl.program_id(0)
    rows = out_ref.shape[0]

    @pl.when(block == 0)
    def _():
        part = width // 3
        for third in range(3):
            for i in range(3):
                joined[i, :, third * part : (third + 1) * part] = grads[3 * third + i][...]
        grad = first_ref[...]
        for i, weight in enumerate((wq, wk, wv)):
            grad = grad + dot(joined[i], weight[...], NT)
        hi = grad.astype(bf16)
        hi_ref[...] = hi
        lo_ref[...] = (grad - hi.astype(f32)).astype(bf16)

    target = lax.broadcasted_iota(jnp.int32, (rows, total), 0) + block * rows
    place = jnp.where(target == src_row[...], 1.0, 0.0).astype(bf16)
    out_ref[...] = dot(place, hi_ref[...]) + dot(place, lo_ref[...])


def input_grad(src_row, first, weights, grads, deps=(), tile=512):
    total, width = first.shape
    flat = [a for group in grads for a in group]
    return pl.pallas_call(
        ignoring(input_grad_kernel, 5 + len(flat), len(deps)),
        grid=(total // tile,),
        in_specs=[whole(src_row.shape), whole((total, width))] + [whole((width, width))] * 3
        + [whole((total, width // 3))] * len(flat) + [ANY] * len(deps),
        out_specs=pl.BlockSpec((tile, width), lambda i: (i, 0)),
        out_shape=shape_of((total, width), f32),
        scratch_shapes=[pltpu.VMEM((3, total, width), bf16), pltpu.VMEM((total, width), bf16), pltpu.VMEM((total, width), bf16)],
        compiler_params=params(52),
        cost_estimate=SHORT,
        name="input_grad",
    )(src_row, first, *weights, *flat, *deps)


def finish_feed_kernel(sc, f0, f1, f2, f3, gi, gu):
    rows, width = gi.shape[0], gu.shape[1]
    for slot, ref in enumerate((f0, f1, f2, f3)):
        quarter = sc[0] ^ slot
        gi[:, pl.ds(pl.multiple_of(quarter * width, 128), width)] = ref[0].astype(f32)
        gu[pl.ds(pl.multiple_of(quarter * rows, 8), rows), :] = ref[1].astype(f32)


def finish_feed(sc, parts, rows, width):
    shapes = [(rows, WIDTHS * width), (WIDTHS * rows, width)]
    return pl.pallas_call(
        finish_feed_kernel,
        in_specs=[SMEM] + [whole(a.shape) for a in parts],
        out_specs=[whole(s) for s in shapes],
        out_shape=[shape_of(s, f32) for s in shapes],
        compiler_params=params(24),
        cost_estimate=SHORT,
        name="finish_feed",
    )(sc, *parts)


def finish_kernel(sc, *refs):
    lows, highs, matrices, vectors = refs[:4], refs[4:8], refs[8:12], refs[12:]
    rows, width = matrices[0].shape
    cut = lows[0].shape[1]
    size = rows * 12 // 4
    for own in range(WIDTHS):

        @pl.when(sc[0] == own)
        def _():
            line = []
            for matrix, ref in enumerate(matrices):
                low, high = lows[matrix ^ own], highs[matrix ^ own]
                ref[:, :cut] = low[...].astype(f32)
                ref[:, cut:] = high[:rows, :].astype(f32)
                tail = high[rows : rows + 16, :].astype(f32)
                line += [tail[0:1], tail[1:2, : size - (width - cut)]]
            line = jnp.concatenate(line, axis=1)
            at = 0
            for ref in vectors:
                ref[...] = line[:, at : at + ref.shape[1]]
                at += ref.shape[1]


def finish(sc, lows, highs, rows, width):
    sizes = [rows] * 8 + [WIDTHS * rows]
    shapes = [(rows, width)] * 4 + [(1, n) for n in sizes]
    inputs = [*lows, *highs]
    return pl.pallas_call(
        finish_kernel,
        in_specs=[SMEM] + [whole(a.shape) for a in inputs],
        out_specs=[whole(s) for s in shapes],
        out_shape=[shape_of(s, f32) for s in shapes],
        compiler_params=params(24),
        cost_estimate=SHORT,
        name="finish",
    )(sc, *inputs)


def exchange(value, axis, bits=1):
    size = lax.axis_size(axis)
    return lax.ppermute(value, axis, [(i, i ^ bits) for i in range(size)])


def join_kernel(count, *refs):
    out = refs[-1]
    at = 0
    for ref in refs[:count]:
        size = ref.shape[0]
        out[at : at + size] = ref[...]
        at += size


def join(parts, deps=()):
    shape = (sum(a.shape[0] for a in parts), *parts[0].shape[1:])
    return pl.pallas_call(
        functools.partial(join_kernel, len(parts)),
        in_specs=[whole(a.shape) for a in parts] + [ANY] * len(deps),
        out_specs=whole(shape),
        out_shape=shape_of(shape),
        compiler_params=params(8),
        cost_estimate=SHORT,
        name="join",
    )(*parts, *deps)


def along_z(piece):
    piece = piece[None]
    return [piece] + [exchange(piece, "z", k) for k in (1, 2, 3)]


def add(*terms):
    total = terms[0].astype(f32)
    for term in terms[1:]:
        total = total + term.astype(f32)
    return total.astype(bf16)


def sums_kernel(plan, count, *refs):
    inputs, outputs = refs[:count], refs[-len(plan) :]
    for terms, out in zip(plan, outputs):
        total = 0.0
        for index, start, stop in terms:
            total = total + inputs[index][start:stop].astype(f32)
        out[...] = total.astype(bf16)


def sums(plan, inputs, deps=()):
    shapes = [(t[0][2] - t[0][1], *inputs[t[0][0]].shape[1:]) for t in plan]
    return pl.pallas_call(
        functools.partial(sums_kernel, plan, len(inputs)),
        in_specs=[whole(a.shape) for a in inputs] + [ANY] * len(deps),
        out_specs=[whole(shape) for shape in shapes],
        out_shape=[shape_of(shape) for shape in shapes],
        compiler_params=params(32),
        cost_estimate=SHORT,
        name="sums",
    )(*inputs, *deps)


def swap(keep, send):
    other = exchange(send, "core")
    return add(keep[0], other[0]), add(keep[1], other[1])


def reduce_z(value):
    return add(value[0], *[exchange(value[k], "z", k) for k in (1, 2, 3)])


def spread(value):
    far = exchange(value, "y")
    return value, exchange(value, "core"), far, exchange(far, "core")


def per_device(
    inputs, cotangent, replacement_ids, augmented_count, segment_ids,
    query_weight, key_weight, value_weight, output_weight, inner_weight, outer_weight,
    query_bias, value_bias, output_bias, inner_bias, outer_bias,
    attention_gain, attention_shift, feed_gain, feed_shift,
):
    total, width = inputs.shape[1:]
    group = lax.axis_index(WIDTH)
    groups = lax.axis_size(WIDTH)
    shards = lax.axis_size(DP)
    direct = shards == PIECES and groups == WIDTHS
    rows = query_weight.shape[0]
    piece_rows = width // PIECES
    part = width // 2
    heads = HEADS * (group + 1) // groups
    own, home = (group, lax.axis_index(DP)) if direct else (jnp.zeros_like(group),) * 2
    sc = jnp.stack([own, home, group + 1, heads]).astype(jnp.int32)

    positions = jnp.arange(total, dtype=jnp.int32)
    sources = jnp.where(positions < augmented_count[0, 0], replacement_ids[0], positions)
    docs = doc_table(segment_ids[0, 0])
    mixed = mix(sources[:, None], inputs[0])

    vectors = (query_bias, value_bias, output_bias, attention_gain, attention_shift,
               outer_bias, feed_gain, feed_shift, inner_bias)
    if direct:
        near_piece = pack(sc, query_weight, value_weight)
        near_column = along_z(near_piece)
        inner_near = lax.all_gather(pack_inner(sc, inner_weight, near_piece), DP, axis=0, tiled=True)
        inner_near = inner_near.reshape(PIECES, rows, width)
        key_piece = pack_key(sc, key_weight, vectors, near_column[1])
        key_column = along_z(key_piece)
        near_column = join(near_column, [key_piece])
        near = join([near_column, exchange(near_column, "x")])
        near_parts = spread(near)
        rest = pack_rest(sc, output_weight, outer_weight, near)
        rest = lax.all_gather(rest, ("core", *DP), axis=0, tiled=True).reshape(2, PIECES, -1, width)
        key_column = join(key_column)
        key_near = join([key_column, exchange(key_column, "x")])
        key_parts = [key_near, exchange(key_near, "core")]
        order = jnp.stack([slot_of(p, home) for p in range(PIECES)])
        lines = jnp.take(key_near[:, rows : rows + 3, :].reshape(PIECES, 3 * part), order, axis=0)
        key_base, value_base, query_base = None, 0, rows // 2
        value_parts = query_parts = near_parts
    else:
        everything = lambda a: lax.all_gather(a, DP, axis=0, tiled=True)
        slots = [(s & 3) * 2 + (s >> 2) for s in range(PIECES)]
        by_piece = lambda a: jnp.stack([a.reshape(PIECES, -1, a.shape[-1])[p] for p in slots])
        step = piece_rows // 2
        plain = lambda a: a.reshape(PIECES, -1, a.shape[-1])
        full = [by_piece(everything(a)) for a in (key_weight, value_weight, query_weight)]
        key_parts, value_parts, query_parts = (
            [a[:, (s >> 1) * step : (s >> 1) * step + step, (s & 1) * part : (s & 1) * part + part] for s in range(4)]
            for a in full
        )
        key_base = value_base = query_base = 0
        inner_full = everything(inner_weight)
        inner_parts = [plain(inner_full[:, q * width : (q + 1) * width]) for q in range(WIDTHS)]
        outer_rows, output_rows = plain(everything(outer_weight)), plain(everything(output_weight))
        rest = jnp.stack([
            jnp.concatenate([outer_rows[:, h * 2 * piece_rows : (h + 1) * 2 * piece_rows],
                             output_rows[:, h * step : (h + 1) * step]], 1)
            for h in range(2)
        ])
        lines = jnp.concatenate([everything(a).reshape(PIECES, -1) for a in vectors], 1)
    small = lines[:, :width].reshape(PIECES, 8, piece_rows).transpose(1, 0, 2).reshape(8, width)
    inner_bias_full = lines[:, width:].reshape(WIDTHS, 1, width)
    vec = small[2:]

    *keys, key_full = project(key_base, 1.0, sc, mixed, jnp.zeros((1, width), bf16), key_parts)
    *values, value_full = project(value_base, 1.0, sc, mixed, small[1:2], value_parts)
    *queries, query_full = project(query_base, HEAD_DIM**-0.5, sc, mixed, small[0:1], query_parts)
    qkv = [(queries[third], keys[third], values[third]) for third in range(3)]
    attended = [attend(0, sc, docs, *qkv[0])]
    if direct:
        inner_far = exchange(inner_near, "y")
        attended.append(attend(1, sc, docs, *qkv[1], [attended[0][2]]))
        attended.append(attend(2, sc, docs, *qkv[2], [attended[1][2]]))
        inner_far = join([inner_far], [attended[2][2]])
        inner_parts = inner_near, exchange(inner_near, "core"), inner_far, exchange(inner_far, "core")
    else:
        attended += [attend(third, sc, docs, *qkv[third]) for third in (1, 2)]
    contexts = [a[0] for a in attended]
    out, first, *dctx, flow, dbi, norm_sums, keep_i, send_i, keep_u, send_u = feed(
        sc, mixed, contexts, cotangent[0], inner_bias_full, vec, inner_parts, rest
    )

    def back(third, *deps):
        _, wide, logsums = attended[third]
        *grads, bias = attend_back(
            third, sc, docs, queries[third], keys[third], values[third], dctx[third], wide, logsums, deps)
        return grads, bias

    def bias_lines(*biases):
        bias = jnp.concatenate([a[:2] for a in biases], axis=1)
        vector_grads = jnp.concatenate([bias, norm_sums[:6]])
        return jnp.concatenate(
            [vector_grads.reshape(8, PIECES, -1).transpose(1, 0, 2).reshape(PIECES, width), dbi.reshape(PIECES, -1)], 1)

    def padded(lines):
        lines = lines.astype(bf16).reshape(PIECES, WIDTHS, -1)
        lines = jnp.pad(lines, ((0, 0), (0, 0), (0, 2 * (width // 3) - lines.shape[2])))
        return jnp.pad(lines.reshape(PIECES, WIDTHS, 2, width // 3), ((0, 0), (0, 0), (0, 14), (0, 0)))

    weight_grads = functools.partial(project_grad, sc=sc, mixed=mixed, contexts=contexts, low=flow)
    if direct:
        near_u, far_u = swap(keep_u, send_u)
        near_i, far_i = swap(keep_i, send_i)
        grads0, bias0 = back(0, near_u, far_u, near_i, far_i)
        grads1, bias1 = back(1, bias0)
        keep_low, send_low = weight_grads((0, 1), grads=(grads0, grads1))
        over_u = exchange(jnp.concatenate([near_u[4:], far_u[4:]]), "x")
        over_i = exchange(far_i, "y")
        over_low = exchange(send_low, "core")
        near_u, far_u, near_i, far_i = sums(
            [[(0, 0, 4), (2, 0, 4)], [(1, 0, 4), (2, 4, 8)], [(3, 0, 4), (4, 0, 4)], [(3, 4, 8), (4, 4, 8)]],
            [near_u, far_u, over_u, near_i, over_i], [keep_low])
        grads2, bias2 = back(2, near_u)
        lines = padded(bias_lines(bias0, bias1, bias2))
        over_u, over_i = exchange(far_u, "y"), exchange(far_i, "x")
        part_u, part_i, near_low, far_low = sums(
            [[(0, 0, 4), (1, 0, 4)], [(2, 0, 4), (3, 0, 4)], [(4, 0, 1), (5, 0, 1)], [(4, 1, 2), (5, 1, 2)]],
            [near_u, over_u, near_i, over_i, keep_low, over_low], [bias2])
        over_low = exchange(far_low[0], "y")
        keep_high, send_high = weight_grads((2,), grads=(grads2,), lines=lines, deps=[part_u], plain=True)
        high = sums([[(0, 0, 2), (1, 0, 2)]], [keep_high, exchange(send_high, "core")])[0]
        sent = high.reshape(2 * PIECES, *high.shape[2:])
        input_gradient = input_grad(
            sources[None, :], first, (query_full, key_full, value_full), (grads0, grads1, grads2), [high])
        near_low, far_low = sums(
            [[(0, 0, 4), (1, 0, 4)], [(0, 4, 8), (1, 4, 8)]], [near_low[0], over_low], [input_gradient])
        over_low = exchange(far_low, "x")
        part_u, part_i = (
            sums([[(0, 0, 1)] + [(k, 0, 1) for k in (1, 2, 3)]],
                 [part[:1]] + [exchange(part[k : k + 1], "z", k) for k in (1, 2, 3)], [input_gradient])[0]
            for part in (part_u, part_i)
        )
        high = lax.all_to_all(sent, ("y", *DP), 0, 0)
        feed_sums = spread(jnp.concatenate([part_i, part_u]))
        part_low = sums([[(0, 0, 4), (1, 0, 4)]], [near_low, over_low], [input_gradient])[0]
        low_sums = spread(reduce_z(part_low))
        high_sums = spread(jnp.sum(high.astype(f32), axis=0).astype(bf16))
        gi, gu = finish_feed(sc, feed_sums, rows, width)
        results = finish(sc, low_sums, high_sums, rows, width)
        gq, gk, gv, go = results[:4]
        bq, bv, bo, ga, sa, bu, gf, sf, bi = (a[0] for a in results[4:])
    else:
        grads, biases = zip(*[back(third) for third in range(3)])
        packs = weight_grads((0, 1), grads=grads[:2]), weight_grads((2,), grads=grads[2:])
        input_gradient = input_grad(sources[None, :], first, (query_full, key_full, value_full), grads)
        ordered = [(p & 1) * 4 + (p >> 1) for p in range(PIECES)]
        in_order = lambda a: jnp.stack([a[s] for s in ordered])
        summed = lambda a: lax.psum(lax.psum_scatter(a, DP, scatter_dimension=0, tiled=True), WIDTH)
        total_sum = lambda a: summed(a.astype(f32))
        quarters_i = [keep_i[0], send_i[0], keep_i[1], send_i[1]]
        blocks_u = [keep_u[0], send_u[0], keep_u[1], send_u[1]]
        gi = total_sum(jnp.concatenate([in_order(a).reshape(width, width) for a in quarters_i], 1))
        gu = total_sum(jnp.stack([in_order(a) for a in blocks_u], 1).reshape(-1, width))
        gq, gk, gv, go = (
            total_sum(jnp.concatenate([in_order(packs[h][side][row]).reshape(width, -1) for h in range(2)], 1))
            for row, side in ((0, 0), (0, 1), (1, 0), (1, 1))
        )
        rows_of = bias_lines(*biases)
        vector_sums = rows_of[:, :width].reshape(PIECES, 8, piece_rows).transpose(1, 0, 2).reshape(8, width)
        bq, bv, bo, ga, sa, bu, gf, sf = (total_sum(a) for a in vector_sums)
        bi = total_sum(dbi.reshape(-1))
    return (out[None], input_gradient[None], gq, gk, gv, go, gi, gu, bq, bv, bo, bi, bu, ga, sa, gf, sf)


def solution(mesh):
    groups, shards = mesh.shape["width"], mesh.shape["dp"]
    fine = jax.sharding.Mesh(mesh.devices.reshape(groups // 2, 2, shards // 2, 2), (*WIDTH, *DP))
    tokens = (P(WIDTH, DP, None),) * 2 + (P(WIDTH, DP),) * 2 + (P(WIDTH, DP, None),)
    matrices = (P(DP, None),) * 6
    vectors = (P(DP),) * 9
    return jax.shard_map(
        per_device,
        mesh=fine,
        in_specs=tokens + matrices + vectors,
        out_specs=(P(WIDTH, DP, None),) * 2 + matrices + vectors,
        check_vma=False,
    )
```

```python
import functools

import jax
import jax.numpy as jnp
from jax import lax
from jax.experimental import pallas as pl
from jax.experimental.pallas import tpu as pltpu
from jax.sharding import PartitionSpec as P

HEADS = 12
HEAD_DIM = 64
EPSILON = 1e-12
NEGATIVE = -1000000000.0
DOCS = 4
LONGEST = 512
BIG = float(2**30)
PIECES = 8
WIDTH = ("y", "core")
DP = ("z", "x")
WIDTHS = 4
bf16 = jnp.bfloat16
f32 = jnp.float32
MIB = 2**20
NN = (((1,), (0,)), ((), ()))
NT = (((1,), (1,)), ((), ()))
TN = (((0,), (0,)), ((), ()))
SMEM = pl.BlockSpec(memory_space=pltpu.SMEM)
ANY = pl.BlockSpec(memory_space=pl.ANY)


def dot(a, b, dims=NN):
    return lax.dot_general(a, b, dims, preferred_element_type=f32)


def params(mib):
    return pltpu.CompilerParams(vmem_limit_bytes=mib * MIB)


SHORT = pl.CostEstimate(flops=1, bytes_accessed=1, transcendentals=0)


def ignoring(kernel, at, count):
    return lambda *refs: kernel(*refs[:at], *refs[at + count :])


def whole(shape):
    return pl.BlockSpec(shape, lambda *_: (0,) * len(shape))


def shape_of(shape, kind=bf16):
    return jax.ShapeDtypeStruct(shape, kind)


def slot_of(piece, home):
    return ((piece & 1) ^ (home & 1)) * 4 + ((piece >> 1) ^ (home >> 1))


def mix_kernel(src_ref, x_ref, mixed_ref):
    rows, total = src_ref.shape[0], x_ref.shape[0]
    pick = src_ref[...] == lax.broadcasted_iota(jnp.int32, (rows, total), 1)
    mixed_ref[...] = dot(jnp.where(pick, 1.0, 0.0).astype(bf16), x_ref[...]).astype(bf16)


def mix(src_col, x):
    total, width = x.shape
    return pl.pallas_call(
        mix_kernel,
        in_specs=[whole((total, 1)), whole((total, width))],
        out_specs=whole((total, width)),
        out_shape=shape_of((total, width)),
        compiler_params=params(24),
        cost_estimate=SHORT,
        name="mix",
    )(src_col, x)


def pack_kernel(sc, wq, wv, near_ref):
    half, part = wq.shape[0] // 2, wq.shape[1] // 2
    rows = pl.ds(pl.multiple_of((sc[0] >> 1) * half, 16), half)
    lanes = pl.ds(pl.multiple_of((sc[0] & 1) * part, 128), part)
    near_ref[:half, :] = wv[rows, lanes]
    near_ref[half:, :] = wq[rows, lanes]


def pack(sc, wq, wv):
    rows, width = wq.shape
    shape = rows, width // 2
    return pl.pallas_call(
        pack_kernel,
        in_specs=[SMEM, whole(wq.shape), whole(wv.shape)],
        out_specs=whole(shape),
        out_shape=shape_of(shape),
        compiler_params=params(8),
        cost_estimate=SHORT,
        name="pack",
    )(sc, wq, wv)


def pack_key_kernel(sc, wk, *refs):
    vectors, key_ref = refs[:9], refs[-1]
    rows, part = wk.shape[0], wk.shape[1] // 2
    line = jnp.concatenate([ref[...].astype(f32) for ref in vectors], axis=1)
    lines = [line[:, i * part : (i + 1) * part] for i in range(3)] + [jnp.zeros((13, part), f32)]
    key_ref[:rows, :] = wk[:, pl.ds(pl.multiple_of((sc[0] & 1) * part, 128), part)]
    key_ref[rows:, :] = jnp.concatenate(lines, axis=0).astype(bf16)


def pack_key(sc, wk, vectors, dep):
    rows, width = wk.shape
    lines = [v[None] for v in vectors]
    shape = rows + 16, width // 2
    return pl.pallas_call(
        ignoring(pack_key_kernel, 2 + len(lines), 1),
        in_specs=[SMEM] + [whole(a.shape) for a in (wk, *lines)] + [ANY],
        out_specs=whole(shape),
        out_shape=shape_of(shape),
        compiler_params=params(8),
        cost_estimate=SHORT,
        name="pack_key",
    )(sc, wk, *lines, dep)


def pack_rest_kernel(sc, wi, wo, wu, rest_ref):
    rows, width = wo.shape
    core = sc[0] & 1
    for quarter in range(2):
        at = pl.multiple_of((2 * core + quarter) * width, 128)
        rest_ref[quarter * rows : (quarter + 1) * rows, :] = wi[:, pl.ds(at, width)]
    rest_ref[2 * rows : 4 * rows, :] = wu[pl.ds(pl.multiple_of(core * 2 * rows, 16), 2 * rows), :]
    rest_ref[4 * rows :, :] = wo[pl.ds(pl.multiple_of(core * (rows // 2), 16), rows // 2), :]


def pack_rest(sc, wi, wo, wu, dep):
    rows, width = wo.shape
    shape = rows * 9 // 2, width
    return pl.pallas_call(
        ignoring(pack_rest_kernel, 4, 1),
        in_specs=[SMEM, whole(wi.shape), whole(wo.shape), whole(wu.shape), ANY],
        out_specs=whole(shape),
        out_shape=shape_of(shape),
        compiler_params=params(8),
        cost_estimate=SHORT,
        name="pack_rest",
    )(sc, wi, wo, wu, dep)


def fetch_parts(sc, sources, base, weight, sem):
    rows, part = weight.shape[0] // PIECES, weight.shape[1] // 2
    step = rows // 2
    for slot, source in enumerate(sources):
        where = sc[0] ^ slot
        at = pl.multiple_of((where & 1) * part, 128)
        for piece in range(PIECES):
            to = pl.multiple_of(piece * rows + (where >> 1) * step, 16)
            pltpu.make_async_copy(
                source.at[slot_of(piece, sc[1]), pl.ds(base, step), :],
                weight.at[pl.ds(to, step), pl.ds(at, part)],
                sem,
            ).start()


def fetch_halves(sc, sources, weight, sem):
    rows, part = weight.shape[0] // PIECES, weight.shape[1] // 2
    for other, source in enumerate(sources):
        at = pl.multiple_of(((sc[0] & 1) ^ other) * part, 128)
        for piece in range(PIECES):
            pltpu.make_async_copy(
                source.at[slot_of(piece, sc[1]), pl.ds(0, rows), :],
                weight.at[pl.ds(piece * rows, rows), pl.ds(at, part)],
                sem,
            ).start()


def project_kernel(fetch, scale, sc, mixed_ref, bias_ref, *refs):
    parts, outs, (weight, sem) = refs[:-5], refs[-5:-2], refs[-2:]
    fetch(sc, parts, weight, sem)
    pltpu.make_async_copy(weight, weight, sem).wait()
    for start in range(0, mixed_ref.shape[0], 512):
        rows = pl.ds(start, 512)
        out = dot(mixed_ref[rows, :], weight[...]) + bias_ref[...].astype(f32)
        out = out.astype(bf16) * jnp.asarray(scale, bf16)
        for third, ref in enumerate(outs):
            size = ref.shape[1]
            ref[rows, :] = out[:, third * size : (third + 1) * size]


def project(base, scale, sc, mixed, bias, parts):
    total, width = mixed.shape
    fetch = fetch_halves if base is None else lambda sc, parts, weight, sem: fetch_parts(sc, parts, base, weight, sem)
    return pl.pallas_call(
        functools.partial(project_kernel, fetch, scale),
        in_specs=[SMEM, whole((total, width)), whole((1, width))] + [ANY] * len(parts),
        out_specs=[whole((total, width // 3))] * 3 + [whole((width, width))],
        out_shape=[shape_of((total, width // 3))] * 3 + [shape_of((width, width))],
        scratch_shapes=[pltpu.SemaphoreType.DMA],
        compiler_params=params(24),
        cost_estimate=SHORT,
        name="project",
    )(sc, mixed, bias, *parts)


def doc_table(segments):
    number = jnp.arange(DOCS)[:, None]
    return jnp.stack([
        jnp.sum((segments[None, :] < number).astype(jnp.int32), axis=1),
        jnp.sum((segments[None, :] == number).astype(jnp.int32), axis=1),
    ])


def head_rows(value):
    lane = lax.broadcasted_iota(jnp.int32, value.shape, 1)
    none = jnp.zeros_like(value)
    return jnp.concatenate(
        [jnp.where(lane < HEAD_DIM, value, none), jnp.where(lane < HEAD_DIM, none, value)], axis=0
    )


def over_docs(docs, sizes, run):
    @pl.loop(0, DOCS)
    def _(doc):
        start, length = docs[0, doc], docs[1, doc]
        low = 0
        for size in sizes:

            @pl.when((length > low) & (length <= size))
            def _():
                run(start, length, size)

            low = size


def mask_columns(length, queries, keys):
    lane = lax.broadcasted_iota(jnp.int32, (keys, 128), 1)
    row = lax.broadcasted_iota(jnp.int32, (keys, 128), 0)
    of_keys = jnp.where((lane == 0) & (row >= length), 1.0, 0.0).astype(bf16)
    lane = lax.broadcasted_iota(jnp.int32, (queries, 128), 1)
    return jnp.where(lane == 0, -BIG, 0.0).astype(bf16), of_keys


def unpack(pairs, total, moves):
    for pair in range(pairs):
        for source, to in moves:
            to[pair, :total, :] = source[:, 128 * pair : 128 * (pair + 1)].astype(f32)
            to[pair, total:, :] = jnp.zeros((LONGEST, 128), f32)


def attend_kernel(first, pairs, sc, docs, q_ref, k_ref, v_ref, ctx_ref, wide_ref, lse_ref, qs, ks, vs, cs, ls):
    total = q_ref.shape[0]
    left = sc[3] - 2 * first
    step = 256

    @pl.when(left <= 0)
    def _():
        for ref in (ctx_ref, wide_ref, lse_ref):
            ref[...] = jnp.zeros_like(ref)

    @pl.when(left > 0)
    def _():
        unpack(pairs, total, ((q_ref, qs), (k_ref, ks), (v_ref, vs)))
        lane = lax.broadcasted_iota(jnp.int32, (step, 128), 1)

        def run(start, length, size):
            @pl.loop(0, (length + step - 1) // step)
            def _(block):
                rows, keys = pl.ds(start + block * step, step), pl.ds(start, size)
                of_queries, of_keys = mask_columns(length, 2 * step, size)
                stat = jnp.zeros((step, 128), f32)
                for pair in range(pairs):
                    queries = jnp.concatenate([head_rows(qs[pair, rows, :].astype(bf16)), of_queries], axis=1)
                    s = dot(queries, jnp.concatenate([ks[pair, keys, :].astype(bf16), of_keys], axis=1), NT)
                    top = jnp.max(s, axis=1, keepdims=True)
                    e = jnp.exp(s - top).astype(bf16)
                    values = jnp.concatenate([vs[pair, keys, :].astype(bf16), jnp.ones((size, 128), bf16)], axis=1)
                    out = dot(e, values)
                    norm = out[:, 128:129]
                    out = out[:, :128] * (1.0 / norm)
                    cs[pair, rows, :] = jnp.where(lane < HEAD_DIM, out[:step], out[step:])
                    logsum = top + jnp.log(norm)
                    stat = jnp.where(
                        lane == 2 * pair, logsum[:step], jnp.where(lane == 2 * pair + 1, logsum[step:], stat)
                    )
                ls[rows, :] = stat

        over_docs(docs, (256, 512), run)
        lane = lax.broadcasted_iota(jnp.int32, (total, 128), 1)
        for pair in range(pairs):
            lanes = slice(128 * pair, 128 * (pair + 1))
            value = jnp.where(lane < (left - 2 * pair) * HEAD_DIM, cs[pair, :total, :], 0.0)
            wide_ref[:, lanes] = value
            ctx_ref[:, lanes] = value.astype(bf16)
        lse_ref[...] = ls[:total, :]


def attend(third, sc, docs, q, k, v, deps=()):
    total, width = q.shape
    pairs = width // 128
    cols = out = whole((total, width))
    return pl.pallas_call(
        ignoring(functools.partial(attend_kernel, pairs * third, pairs), 5, len(deps)),
        in_specs=[SMEM, SMEM, cols, cols, cols] + [ANY] * len(deps),
        out_specs=[out, out, whole((total, 128))],
        out_shape=[shape_of((total, width)), shape_of((total, width), f32), shape_of((total, 128), f32)],
        scratch_shapes=[pltpu.VMEM((pairs, total + LONGEST, 128), f32)] * 4 + [pltpu.VMEM((total + LONGEST, 128), f32)],
        compiler_params=params(32),
        cost_estimate=SHORT,
        name="attend",
    )(sc, docs, q, k, v, *deps)


def attend_back_kernel(
    first, pairs, sc, docs, q_ref, k_ref, v_ref, c_ref, wide_ref, lse_ref,
    dq_ref, dk_ref, dv_ref, sums_ref, qs, ks, vs, cs, xs, ls,
):
    total = q_ref.shape[0]
    left = sc[3] - 2 * first

    @pl.when(left <= 0)
    def _():
        for ref in (dq_ref, dk_ref, dv_ref, sums_ref):
            ref[...] = jnp.zeros_like(ref)

    @pl.when(left > 0)
    def _():
        unpack(pairs, total, ((q_ref, qs), (k_ref, ks), (v_ref, vs), (c_ref, cs), (wide_ref, xs)))
        ls[:total, :] = lse_ref[...]
        ls[total:, :] = jnp.zeros((LONGEST, 128), f32)

        def run(start, length, size):
            rows = pl.ds(start, size)
            lane = lax.broadcasted_iota(jnp.int32, (size, 128), 1)
            live = lax.broadcasted_iota(jnp.int32, (size, 128), 0) < length
            of_queries, of_keys = mask_columns(length, 2 * size, size)
            logsums = jnp.where(live, ls[rows, :], BIG)
            for pair in range(pairs):
                queries = head_rows(qs[pair, rows, :].astype(bf16))
                grad = jnp.where(live, cs[pair, rows, :], 0.0)
                grads = head_rows(grad.astype(bf16))
                inner = grad * xs[pair, rows, :]
                delta = jnp.concatenate([
                    jnp.sum(jnp.where(lane < HEAD_DIM, inner, 0.0), axis=1, keepdims=True),
                    jnp.sum(jnp.where(lane < HEAD_DIM, 0.0, inner), axis=1, keepdims=True),
                ], axis=0)
                logsum = jnp.concatenate(
                    [logsums[:, 2 * pair : 2 * pair + 1], logsums[:, 2 * pair + 1 : 2 * pair + 2]], axis=0
                )
                keys = ks[pair, rows, :].astype(bf16)
                s = dot(jnp.concatenate([queries, of_queries], axis=1), jnp.concatenate([keys, of_keys], axis=1), NT)
                dp = dot(grads, vs[pair, rows, :].astype(bf16), NT)
                p = jnp.exp(s - logsum)
                ds = (p * (dp - delta)).astype(bf16)
                dv = dot(p.astype(bf16), grads, TN)
                dk = dot(ds, queries, TN)
                dq = dot(ds, keys)
                dq = jnp.where(lane < HEAD_DIM, dq[:size], dq[size:]) * HEAD_DIM**-0.5
                qs[pair, rows, :] = jnp.where(live, dq, qs[pair, rows, :])
                ks[pair, rows, :] = jnp.where(live, dk, ks[pair, rows, :])
                vs[pair, rows, :] = jnp.where(live, dv, vs[pair, rows, :])

        over_docs(docs, (128, 256, 384, 512), run)
        for pair in range(pairs):
            lanes = slice(128 * pair, 128 * (pair + 1))
            for to, value in ((dq_ref, qs), (dk_ref, ks), (dv_ref, vs)):
                to[:, lanes] = value[pair, :total, :].astype(bf16)
        sums_ref[0:1, :] = col_sum(dq_ref[...].astype(f32))
        sums_ref[1:2, :] = col_sum(dv_ref[...].astype(f32))


def attend_back(third, sc, docs, q, k, v, c, wide, lse, deps=()):
    total, width = q.shape
    pairs = width // 128
    cols = out = whole((total, width))
    return pl.pallas_call(
        ignoring(functools.partial(attend_back_kernel, pairs * third, pairs), 8, len(deps)),
        in_specs=[SMEM, SMEM, cols, cols, cols, cols, out, whole((total, 128))] + [ANY] * len(deps),
        out_specs=[out] * 3 + [whole((8, width))],
        out_shape=[shape_of((total, width))] * 3 + [shape_of((8, width), f32)],
        scratch_shapes=[pltpu.VMEM((pairs, total + LONGEST, 128), f32)] * 5 + [pltpu.VMEM((total + LONGEST, 128), f32)],
        compiler_params=params(40),
        cost_estimate=SHORT,
        name="attend_back",
    )(sc, docs, q, k, v, c, wide, lse, *deps)


def row_mean(value):
    return jnp.mean(value, axis=1, keepdims=True)


def normalise(hidden):
    centred = hidden - row_mean(hidden)
    rate = lax.rsqrt(row_mean(centred * centred) + EPSILON)
    return centred * rate, rate


def norm_back(grad, gain, unit, rate):
    scaled = grad * gain
    return rate * (scaled - row_mean(scaled) - unit * row_mean(scaled * unit))


def col_sum(value):
    return jnp.sum(value, axis=0, keepdims=True)


def feed_kernel(
    sc, mixed_ref, c0, c1, c2, cot_hbm, bi_ref, vec_ref, *refs
):
    rest = refs[0]
    (out_hbm, first_ref, d0, d1, d2, flow_ref, dbi_ref, sums_ref, keep_i, send_i, keep_u, send_u,
     wi, wu, wo, act, slope, unit_ref, grad_ref, low_ref, glow_ref, rate_ref, cot_ref, stage,
     wo_sem, wi_sem, wu_sem, stage_sem, cot_sem, out_sem) = refs[1:]
    total, width = mixed_ref.shape
    unit_rows = width // PIECES
    outer_rows = WIDTHS * width // PIECES
    own, home, active, heads = sc[0], sc[1], sc[2], sc[3]
    ob, g1, s1, ub, g2, s2 = (vec_ref[i : i + 1, :].astype(f32) for i in range(6))

    for half in range(2):
        pltpu.make_async_copy(
            rest.at[half, :, pl.ds(4 * unit_rows, unit_rows // 2), :], wo.at[:, half], wo_sem.at[half]
        ).start()
    for slot in range(WIDTHS):
        quarter = own ^ slot
        at = pl.multiple_of((quarter & 1) * unit_rows, 16)
        pltpu.make_async_copy(
            rest.at[quarter >> 1, :, pl.ds(at, unit_rows), :], wi.at[slot], wi_sem.at[slot]
        ).start()
        for half in range(2):
            pltpu.make_async_copy(
                rest.at[half, pl.ds(2 * quarter, 2), pl.ds(2 * unit_rows, 2 * unit_rows), :],
                wu.at[slot, :, half],
                wu_sem.at[slot, half],
            ).start()
    cot_copy = pltpu.make_async_copy(cot_hbm, cot_ref, cot_sem)
    cot_copy.start()

    def inner_weight(slot):
        return wi[slot].reshape(width, width)

    def outer(slot):
        return wu[slot].reshape(width, width)

    def output():
        return wo[...].reshape(width, width)

    step = 256
    blocks = [pl.ds(i * step, step) for i in range(total // step)]
    for half in range(2):
        pltpu.make_async_copy(wo.at[:, half], wo.at[:, half], wo_sem.at[half]).wait()
    for rows in blocks:
        ctx = jnp.concatenate([c0[rows, :], c1[rows, :], c2[rows, :]], axis=1)
        unit, rate = normalise(mixed_ref[rows, :].astype(f32) + dot(ctx, output()) + ob)
        unit_ref[rows, :] = unit
        rate_ref[rows, :] = rate
        normed = unit * g1 + s1
        low_ref[rows, :] = normed.astype(bf16)
        first_ref[rows, :] = normed + ub
    for slot in range(WIDTHS):
        quarter = own ^ slot
        pltpu.make_async_copy(wi.at[slot], wi.at[slot], wi_sem.at[slot]).wait()
        for half in range(2):
            pltpu.make_async_copy(wu.at[slot, :, half], wu.at[slot, :, half], wu_sem.at[slot, half]).wait()

        @pl.when(quarter < active)
        def _():
            bias = bi_ref[quarter].astype(f32)
            for rows in blocks:
                inner = dot(low_ref[rows, :], inner_weight(slot)) + bias
                phi = 0.5 * (1.0 + lax.erf(inner * 0.7071067811865476))
                act[slot, rows, :] = (inner * phi).astype(bf16)
                density = jnp.exp(-0.5 * inner * inner) * 0.3989422804014327
                slope[slot, rows, :] = (phi + inner * density).astype(bf16)
            first_ref[...] += dot(act[slot], outer(slot))

    sums_ref[...] = jnp.zeros_like(sums_ref)
    cot_copy.wait()
    for rows in blocks:
        unit, rate = normalise(first_ref[rows, :])
        cot = cot_ref[rows, :].astype(f32)
        cot_ref[rows, :] = (unit * g2 + s2).astype(bf16)
        grad = norm_back(cot, g2, unit, rate)
        grad_ref[rows, :] = grad
        low = grad.astype(bf16)
        glow_ref[rows, :] = low
        sums_ref[3:4, :] += col_sum(low.astype(f32))
        sums_ref[4:5, :] += col_sum(cot * unit)
        sums_ref[5:6, :] += col_sum(cot)
    out_copy = pltpu.make_async_copy(cot_ref, out_hbm, out_sem)
    out_copy.start()
    first_ref[...] = grad_ref[...]

    def staged(slot):
        for i in range(2):
            pltpu.make_async_copy(stage.at[slot & 1, i], stage.at[slot & 1, i], stage_sem.at[slot & 1, i]).wait()

    for slot in range(WIDTHS):
        quarter = own ^ slot
        here = slot & 1

        if slot > 1:
            staged(slot)

        @pl.when(quarter >= active)
        def _():
            stage[here] = jnp.zeros((2, width, width), bf16)
            dbi_ref[quarter] = jnp.zeros((1, width), f32)

        @pl.when(quarter < active)
        def _():
            stage[here, 1] = dot(act[slot], glow_ref[...], TN).astype(bf16)
            inner = (dot(glow_ref[...], outer(slot), NT) * slope[slot].astype(f32)).astype(bf16)
            dbi_ref[quarter] = col_sum(inner.astype(f32))
            stage[here, 0] = dot(low_ref[...], inner, TN).astype(bf16)
            first_ref[...] += dot(inner, inner_weight(slot), NT)

        to = (keep_i, send_i)[slot & 1]
        for piece in range(PIECES):
            pltpu.make_async_copy(
                stage.at[here, 0, pl.ds(piece * unit_rows, unit_rows), :],
                to.at[slot >> 1, slot_of(piece, home)],
                stage_sem.at[here, 0],
            ).start()
        for end in range(2):
            for part in range(WIDTHS):
                at = pl.multiple_of(end * outer_rows + (own ^ part) * unit_rows, 16)
                pltpu.make_async_copy(
                    stage.at[here, 1, pl.ds(at, unit_rows), :],
                    (keep_u, send_u)[part & 1].at[part >> 1, slot_of(2 * quarter + end, home)],
                    stage_sem.at[here, 1],
                ).start()

    for rows in blocks:
        unit = unit_ref[rows, :]
        normed_grad = first_ref[rows, :]
        first = norm_back(normed_grad, g1, unit, rate_ref[rows, :])
        first_ref[rows, :] = first
        low = first.astype(bf16)
        flow_ref[rows, :] = low
        dctx = dot(low, output(), NT)
        lane = lax.broadcasted_iota(jnp.int32, dctx.shape, 1)
        dctx = jnp.where(lane < heads * HEAD_DIM, dctx, 0.0).astype(bf16)
        for third, ref in enumerate((d0, d1, d2)):
            size = ref.shape[1]
            ref[rows, :] = dctx[:, third * size : (third + 1) * size]
        sums_ref[0:1, :] += col_sum(low.astype(f32))
        sums_ref[1:2, :] += col_sum(normed_grad * unit)
        sums_ref[2:3, :] += col_sum(normed_grad)
    staged(WIDTHS - 2)
    staged(WIDTHS - 1)
    out_copy.wait()


def feed(sc, mixed, contexts, cot, bi, vec, rest):
    total, width = mixed.shape
    square = whole((total, width))
    piece = (2, PIECES, width // PIECES, width)
    return pl.pallas_call(
        feed_kernel,
        in_specs=[SMEM, square] + [whole((total, width // 3))] * 3 + [ANY, whole(bi.shape), whole(vec.shape)]
        + [ANY],
        out_specs=[ANY, square] + [whole((total, width // 3))] * 3 + [square, whole((WIDTHS, 1, width)), whole((8, width))]
        + [ANY] * 4,
        out_shape=[
            shape_of((total, width)), shape_of((total, width), f32), *[shape_of((total, width // 3))] * 3,
            shape_of((total, width)), shape_of((WIDTHS, 1, width), f32), shape_of((8, width), f32),
        ] + [shape_of(piece)] * 4,
        scratch_shapes=[
            pltpu.VMEM((WIDTHS, PIECES, width // PIECES, width), bf16),
            pltpu.VMEM((WIDTHS, 2, 2, width // 4, width), bf16),
            pltpu.VMEM((PIECES, 2, width // PIECES // 2, width), bf16),
            pltpu.VMEM((WIDTHS, total, width), bf16), pltpu.VMEM((WIDTHS, total, width), bf16),
            pltpu.VMEM((total, width), f32), pltpu.VMEM((total, width), f32),
            pltpu.VMEM((total, width), bf16), pltpu.VMEM((total, width), bf16), pltpu.VMEM((total, 1), f32),
            pltpu.VMEM((total, width), bf16), pltpu.VMEM((2, 2, width, width), bf16),
            pltpu.SemaphoreType.DMA((2,)), pltpu.SemaphoreType.DMA((WIDTHS,)), pltpu.SemaphoreType.DMA((WIDTHS, 2)),
            pltpu.SemaphoreType.DMA((2, 2)), pltpu.SemaphoreType.DMA, pltpu.SemaphoreType.DMA,
        ],
        compiler_params=params(60),
        cost_estimate=SHORT,
        name="feed",
    )(sc, mixed, *contexts, cot, bi, vec, rest)


def project_grad_kernel(thirds, with_lines, sc, mixed_ref, ctx0, ctx1, ctx2, low_ref, *refs):
    grads, lines = refs[: 3 * len(thirds)], refs[3 * len(thirds)] if with_lines else None
    keep, send = refs[-2:]
    total, width = mixed_ref.shape
    part = width // 3
    rows = width // PIECES
    own, home = sc[0], sc[1]
    for matrix in range(4):
        if matrix < 3:
            left = mixed_ref[...]
            right = jnp.concatenate([grads[3 * i + matrix][...] for i in range(len(thirds))], axis=1)
        else:
            left = jnp.concatenate([ctx0[...], ctx1[...], ctx2[...]], axis=1)
            right = low_ref[:, thirds[0] * part : (thirds[-1] + 1) * part]
        value = dot(left, right, TN).astype(bf16)
        slot = matrix ^ own

        def put(ref):
            for piece in range(PIECES):
                side, to = slot >> 1, slot_of(piece, home)
                ref[side, to, pl.ds(0, rows), :] = value[piece * rows : (piece + 1) * rows]
                if with_lines:
                    ref[side, to, pl.ds(rows, 16), :] = lines[piece, matrix]

        @pl.when((slot & 1) == 0)
        def _():
            put(keep)

        @pl.when((slot & 1) == 1)
        def _():
            put(send)


def project_grad(thirds, sc, mixed, contexts, low, grads, lines=None, deps=()):
    total, width = mixed.shape
    part = width // 3
    extra = [] if lines is None else [lines]
    flat = [a for group in grads for a in group]
    pack = (2, PIECES, width // PIECES + 16 * len(extra), part * len(thirds))
    count = 6 + len(flat) + len(extra)
    return pl.pallas_call(
        ignoring(functools.partial(project_grad_kernel, thirds, bool(extra)), count, len(deps)),
        in_specs=[SMEM, whole((total, width))] + [whole((total, part))] * 3 + [whole((total, width))]
        + [whole((total, part))] * len(flat) + [whole(a.shape) for a in extra] + [ANY] * len(deps),
        out_specs=[whole(pack), whole(pack)],
        out_shape=[shape_of(pack), shape_of(pack)],
        compiler_params=params(32),
        cost_estimate=SHORT,
        name="project_grad",
    )(sc, mixed, *contexts, low, *flat, *extra, *deps)


def input_grad_kernel(src_row, first_ref, wq, wk, wv, *refs):
    grads, out_ref, joined, low_ref = refs[:-3], *refs[-3:]
    total, width = first_ref.shape
    block = pl.program_id(0)
    rows = out_ref.shape[0]

    @pl.when(block == 0)
    def _():
        part = width // 3
        for third in range(3):
            for i in range(3):
                joined[i, :, third * part : (third + 1) * part] = grads[3 * third + i][...]
        grad = first_ref[...]
        for i, weight in enumerate((wq, wk, wv)):
            grad = grad + dot(joined[i], weight[...], NT)
        low_ref[...] = grad.astype(bf16)

    target = lax.broadcasted_iota(jnp.int32, (rows, total), 0) + block * rows
    place = jnp.where(target == src_row[...], 1.0, 0.0).astype(bf16)
    out_ref[...] = dot(place, low_ref[...])


def input_grad(src_row, first, weights, grads, deps=(), tile=512):
    total, width = first.shape
    flat = [a for group in grads for a in group]
    return pl.pallas_call(
        ignoring(input_grad_kernel, 5 + len(flat), len(deps)),
        grid=(total // tile,),
        in_specs=[whole(src_row.shape), whole((total, width))] + [whole((width, width))] * 3
        + [whole((total, width // 3))] * len(flat) + [ANY] * len(deps),
        out_specs=pl.BlockSpec((tile, width), lambda i: (i, 0)),
        out_shape=shape_of((total, width), f32),
        scratch_shapes=[pltpu.VMEM((3, total, width), bf16), pltpu.VMEM((total, width), bf16)],
        compiler_params=params(52),
        cost_estimate=SHORT,
        name="input_grad",
    )(src_row, first, *weights, *flat, *deps)


def finish_feed_kernel(sc, f0, f1, f2, f3, gi, gu):
    rows, width = gi.shape[0], gu.shape[1]
    for slot, ref in enumerate((f0, f1, f2, f3)):
        quarter = sc[0] ^ slot
        gi[:, pl.ds(pl.multiple_of(quarter * width, 128), width)] = ref[0].astype(f32)
        gu[pl.ds(pl.multiple_of(quarter * rows, 8), rows), :] = ref[1].astype(f32)


def finish_feed(sc, parts, rows, width):
    shapes = [(rows, WIDTHS * width), (WIDTHS * rows, width)]
    return pl.pallas_call(
        finish_feed_kernel,
        in_specs=[SMEM] + [whole(a.shape) for a in parts],
        out_specs=[whole(s) for s in shapes],
        out_shape=[shape_of(s, f32) for s in shapes],
        compiler_params=params(24),
        cost_estimate=SHORT,
        name="finish_feed",
    )(sc, *parts)


def finish_kernel(cut, sc, *refs):
    parts, matrices, vectors = refs[:4], refs[4:8], refs[8:]
    rows, width = matrices[0].shape
    size = rows * 12 // 4
    for own in range(WIDTHS):

        @pl.when(sc[0] == own)
        def _():
            line = []
            for matrix, ref in enumerate(matrices):
                part = parts[matrix ^ own]
                ref[...] = part[:rows, :].astype(f32)
                tail = part[rows : rows + 16, cut:].astype(f32)
                line += [tail[0:1], tail[1:2, : size - (width - cut)]]
            line = jnp.concatenate(line, axis=1)
            at = 0
            for ref in vectors:
                ref[...] = line[:, at : at + ref.shape[1]]
                at += ref.shape[1]


def finish(sc, parts, rows, width, cut):
    sizes = [rows] * 8 + [WIDTHS * rows]
    shapes = [(rows, width)] * 4 + [(1, n) for n in sizes]
    return pl.pallas_call(
        functools.partial(finish_kernel, cut),
        in_specs=[SMEM] + [whole(a.shape) for a in parts],
        out_specs=[whole(s) for s in shapes],
        out_shape=[shape_of(s, f32) for s in shapes],
        compiler_params=params(24),
        cost_estimate=SHORT,
        name="finish",
    )(sc, *parts)


def exchange(value, axis, bits=1):
    size = lax.axis_size(axis)
    return lax.ppermute(value, axis, [(i, i ^ bits) for i in range(size)])


def join_kernel(count, *refs):
    out = refs[-1]
    at = 0
    for ref in refs[:count]:
        size = ref.shape[0]
        out[at : at + size] = ref[...]
        at += size


def join(parts, deps=()):
    shape = (sum(a.shape[0] for a in parts), *parts[0].shape[1:])
    return pl.pallas_call(
        functools.partial(join_kernel, len(parts)),
        in_specs=[whole(a.shape) for a in parts] + [ANY] * len(deps),
        out_specs=whole(shape),
        out_shape=shape_of(shape),
        compiler_params=params(8),
        cost_estimate=SHORT,
        name="join",
    )(*parts, *deps)


def along_z(piece):
    piece = piece[None]
    return [piece] + [exchange(piece, "z", k) for k in (1, 2, 3)]


def add(*terms):
    total = terms[0].astype(f32)
    for term in terms[1:]:
        total = total + term.astype(f32)
    return total.astype(bf16)


def sums_kernel(plan, count, *refs):
    inputs, outputs = refs[:count], refs[-len(plan) :]
    for blocks, out in zip(plan, outputs):
        for at, terms in blocks:
            total = 0.0
            for index, where in terms:
                total = total + inputs[index][where].astype(f32)
            out[at] = total.astype(bf16)


def sums(plan, shapes, inputs, deps=()):
    return pl.pallas_call(
        functools.partial(sums_kernel, plan, len(inputs)),
        in_specs=[whole(a.shape) for a in inputs] + [ANY] * len(deps),
        out_specs=[whole(shape) for shape in shapes],
        out_shape=[shape_of(shape) for shape in shapes],
        compiler_params=params(32),
        cost_estimate=SHORT,
        name="sums",
    )(*inputs, *deps)


def swap(keep, send):
    other = exchange(send, "core")
    return add(keep[0], other[0]), add(keep[1], other[1])


def spread(value):
    far = exchange(value, "y")
    return value, exchange(value, "core"), far, exchange(far, "core")


def per_device(
    inputs, cotangent, replacement_ids, augmented_count, segment_ids,
    query_weight, key_weight, value_weight, output_weight, inner_weight, outer_weight,
    query_bias, value_bias, output_bias, inner_bias, outer_bias,
    attention_gain, attention_shift, feed_gain, feed_shift,
):
    total, width = inputs.shape[1:]
    group = lax.axis_index(WIDTH)
    groups = lax.axis_size(WIDTH)
    shards = lax.axis_size(DP)
    direct = shards == PIECES and groups == WIDTHS
    rows = query_weight.shape[0]
    piece_rows = width // PIECES
    part = width // 2
    heads = HEADS * (group + 1) // groups
    own, home = (group, lax.axis_index(DP)) if direct else (jnp.zeros_like(group),) * 2
    sc = jnp.stack([own, home, group + 1, heads]).astype(jnp.int32)

    positions = jnp.arange(total, dtype=jnp.int32)
    sources = jnp.where(positions < augmented_count[0, 0], replacement_ids[0], positions)
    docs = doc_table(segment_ids[0, 0])
    mixed = mix(sources[:, None], inputs[0])

    vectors = (query_bias, value_bias, output_bias, attention_gain, attention_shift,
               outer_bias, feed_gain, feed_shift, inner_bias)
    if direct:
        near_piece = pack(sc, query_weight, value_weight)
        near_column = along_z(near_piece)
        rest = pack_rest(sc, inner_weight, output_weight, outer_weight, near_piece)
        rest = lax.all_gather(rest, ("core", *DP), axis=0, tiled=True).reshape(2, PIECES, -1, width)
        key_piece = pack_key(sc, key_weight, vectors, near_column[1])
        key_column = along_z(key_piece)
        near_column = join(near_column, [key_piece])
        near = join([near_column, exchange(near_column, "x")])
        near_parts = spread(near)
        key_column = join(key_column)
        key_near = join([key_column, exchange(key_column, "x")])
        key_parts = [key_near, exchange(key_near, "core")]
        order = jnp.stack([slot_of(p, home) for p in range(PIECES)])
        lines = jnp.take(key_near[:, rows : rows + 3, :].reshape(PIECES, 3 * part), order, axis=0)
        key_base, value_base, query_base = None, 0, rows // 2
        value_parts = query_parts = near_parts
    else:
        everything = lambda a: lax.all_gather(a, DP, axis=0, tiled=True)
        slots = [(s & 3) * 2 + (s >> 2) for s in range(PIECES)]
        by_piece = lambda a: jnp.stack([a.reshape(PIECES, -1, a.shape[-1])[p] for p in slots])
        step = piece_rows // 2
        plain = lambda a: a.reshape(PIECES, -1, a.shape[-1])
        full = [by_piece(everything(a)) for a in (key_weight, value_weight, query_weight)]
        key_parts, value_parts, query_parts = (
            [a[:, (s >> 1) * step : (s >> 1) * step + step, (s & 1) * part : (s & 1) * part + part] for s in range(4)]
            for a in full
        )
        key_base = value_base = query_base = 0
        inner_full = plain(everything(inner_weight))
        outer_rows, output_rows = plain(everything(outer_weight)), plain(everything(output_weight))
        rest = jnp.stack([
            jnp.concatenate([
                inner_full[:, :, 2 * h * width : (2 * h + 1) * width],
                inner_full[:, :, (2 * h + 1) * width : (2 * h + 2) * width],
                outer_rows[:, h * 2 * piece_rows : (h + 1) * 2 * piece_rows],
                output_rows[:, h * step : (h + 1) * step],
            ], 1)
            for h in range(2)
        ])
        lines = jnp.concatenate([everything(a).reshape(PIECES, -1) for a in vectors], 1)
    small = lines[:, :width].reshape(PIECES, 8, piece_rows).transpose(1, 0, 2).reshape(8, width)
    inner_bias_full = lines[:, width:].reshape(WIDTHS, 1, width)
    vec = small[2:]

    *keys, key_full = project(key_base, 1.0, sc, mixed, jnp.zeros((1, width), bf16), key_parts)
    *values, value_full = project(value_base, 1.0, sc, mixed, small[1:2], value_parts)
    *queries, query_full = project(query_base, HEAD_DIM**-0.5, sc, mixed, small[0:1], query_parts)
    qkv = [(queries[third], keys[third], values[third]) for third in range(3)]
    attended = [attend(0, sc, docs, *qkv[0])]
    for third in (1, 2):
        attended.append(attend(third, sc, docs, *qkv[third], [attended[-1][2]]))
    contexts = [a[0] for a in attended]
    out, first, *dctx, flow, dbi, norm_sums, keep_i, send_i, keep_u, send_u = feed(
        sc, mixed, contexts, cotangent[0], inner_bias_full, vec, rest
    )

    def back(third, *deps):
        _, wide, logsums = attended[third]
        *grads, bias = attend_back(
            third, sc, docs, queries[third], keys[third], values[third], dctx[third], wide, logsums, deps)
        return grads, bias

    def bias_lines(*biases):
        bias = jnp.concatenate([a[:2] for a in biases], axis=1)
        vector_grads = jnp.concatenate([bias, norm_sums[:6]])
        return jnp.concatenate(
            [vector_grads.reshape(8, PIECES, -1).transpose(1, 0, 2).reshape(PIECES, width), dbi.reshape(PIECES, -1)], 1)

    def padded(lines):
        lines = lines.astype(bf16).reshape(PIECES, WIDTHS, -1)
        lines = jnp.pad(lines, ((0, 0), (0, 0), (0, 2 * (width // 3) - lines.shape[2])))
        return jnp.pad(lines.reshape(PIECES, WIDTHS, 2, width // 3), ((0, 0), (0, 0), (0, 14), (0, 0)))

    weight_grads = functools.partial(project_grad, sc=sc, mixed=mixed, contexts=contexts, low=flow)
    if direct:
        near_u, far_u = swap(keep_u, send_u)
        near_i, far_i = swap(keep_i, send_i)
        grads0, bias0 = back(0, near_u, far_u, near_i, far_i)
        grads1, bias1 = back(1, bias0)
        keep_low, send_low = weight_grads((0, 1), grads=(grads0, grads1))
        over_u = exchange(jnp.concatenate([near_u[4:], far_u[4:]]), "x")
        over_i = exchange(far_i, "y")
        over_low = exchange(send_low, "core")
        front, back_half, all_of = slice(0, 4), slice(4, 8), slice(None)
        quad = (4, piece_rows, width)
        near_u, far_u, near_i, far_i = sums(
            [[(all_of, [(0, front), (2, front)])], [(all_of, [(1, front), (2, back_half)])],
             [(all_of, [(3, front), (4, front)])], [(all_of, [(3, back_half), (4, back_half)])]],
            [quad] * 4, [near_u, far_u, over_u, near_i, over_i], [keep_low])
        grads2, bias2 = back(2, near_u)
        lines = padded(bias_lines(bias0, bias1, bias2))
        over_u, over_i = exchange(far_u, "y"), exchange(far_i, "x")
        cols = keep_low.shape[3]
        octet = (PIECES, piece_rows, cols)
        column, near_low, far_low = sums(
            [[((all_of, 0), [(2, all_of), (3, all_of)]), ((all_of, 1), [(0, all_of), (1, all_of)])],
             [(all_of, [(4, 0), (5, 0)])], [(all_of, [(4, 1), (5, 1)])]],
            [(4, 2, piece_rows, width), octet, octet],
            [near_u, over_u, near_i, over_i, keep_low, over_low], [bias2])
        over_low = exchange(far_low, "y")
        columns = [column[:1]] + [exchange(column[k : k + 1], "z", k) for k in (1, 2, 3)]
        keep_high, send_high = weight_grads((2,), grads=(grads2,), lines=lines, deps=[column])
        tall, rest_cols = keep_high.shape[2:]
        octet = (PIECES, tall, rest_cols)
        near_high, far_high, sent = sums(
            [[(all_of, [(0, 0), (1, 0)])], [(all_of, [(0, 1), (1, 1)])],
             [(front, [(0, (0, back_half)), (1, (0, back_half))]), (back_half, [(0, (1, back_half)), (1, (1, back_half))])]],
            [octet] * 3, [keep_high, exchange(send_high, "core")])
        over_high = exchange(sent, "x")
        input_gradient = input_grad(
            sources[None, :], first, (query_full, key_full, value_full), (grads0, grads1, grads2), [sent])
        feed_sum, = sums([[(all_of, [(k, 0) for k in range(4)])]], [(2, piece_rows, width)], columns)
        feed_sums = spread(feed_sum)
        near_low, far_low, near_high, far_high = sums(
            [[(all_of, [(0, front), (1, front)])], [(all_of, [(0, back_half), (1, back_half)])],
             [(all_of, [(2, front), (4, front)])], [(all_of, [(3, front), (4, back_half)])]],
            [(4, piece_rows, cols)] * 2 + [(4, tall, rest_cols)] * 2,
            [near_low, over_low, near_high, far_high, over_high], [input_gradient, feed_sum])
        over_low, over_high = exchange(far_low, "x"), exchange(far_high, "y")
        left, right, top = slice(0, cols), slice(cols, width), slice(0, piece_rows)
        column, = sums(
            [[((all_of, top, left), [(0, all_of), (1, all_of)]), ((all_of, all_of, right), [(2, all_of), (3, all_of)])]],
            [(4, tall, width)], [near_low, over_low, near_high, over_high])
        columns = [column[:1]] + [exchange(column[k : k + 1], "z", k) for k in (1, 2, 3)]
        head_sum, = sums([[(all_of, [(k, 0) for k in range(4)])]], [(tall, width)], columns)
        head_sums = spread(head_sum)
        gi, gu = finish_feed(sc, feed_sums, rows, width)
        results = finish(sc, head_sums, rows, width, cols)
        gq, gk, gv, go = results[:4]
        bq, bv, bo, ga, sa, bu, gf, sf, bi = (a[0] for a in results[4:])
    else:
        grads, biases = zip(*[back(third) for third in range(3)])
        packs = weight_grads((0, 1), grads=grads[:2]), weight_grads((2,), grads=grads[2:])
        input_gradient = input_grad(sources[None, :], first, (query_full, key_full, value_full), grads)
        ordered = [(p & 1) * 4 + (p >> 1) for p in range(PIECES)]
        in_order = lambda a: jnp.stack([a[s] for s in ordered])
        summed = lambda a: lax.psum(lax.psum_scatter(a, DP, scatter_dimension=0, tiled=True), WIDTH)
        total_sum = lambda a: summed(a.astype(f32))
        quarters_i = [keep_i[0], send_i[0], keep_i[1], send_i[1]]
        blocks_u = [keep_u[0], send_u[0], keep_u[1], send_u[1]]
        gi = total_sum(jnp.concatenate([in_order(a).reshape(width, width) for a in quarters_i], 1))
        gu = total_sum(jnp.stack([in_order(a) for a in blocks_u], 1).reshape(-1, width))
        gq, gk, gv, go = (
            total_sum(jnp.concatenate([in_order(packs[h][side][row]).reshape(width, -1) for h in range(2)], 1))
            for row, side in ((0, 0), (0, 1), (1, 0), (1, 1))
        )
        rows_of = bias_lines(*biases)
        vector_sums = rows_of[:, :width].reshape(PIECES, 8, piece_rows).transpose(1, 0, 2).reshape(8, width)
        bq, bv, bo, ga, sa, bu, gf, sf = (total_sum(a) for a in vector_sums)
        bi = total_sum(dbi.reshape(-1))
    return (out[None], input_gradient[None], gq, gk, gv, go, gi, gu, bq, bv, bo, bi, bu, ga, sa, gf, sf)


def solution(mesh):
    groups, shards = mesh.shape["width"], mesh.shape["dp"]
    fine = jax.sharding.Mesh(mesh.devices.reshape(groups // 2, 2, shards // 2, 2), (*WIDTH, *DP))
    tokens = (P(WIDTH, DP, None),) * 2 + (P(WIDTH, DP),) * 2 + (P(WIDTH, DP, None),)
    matrices = (P(DP, None),) * 6
    vectors = (P(DP),) * 9
    return jax.shard_map(
        per_device,
        mesh=fine,
        in_specs=tokens + matrices + vectors,
        out_specs=(P(WIDTH, DP, None),) * 2 + matrices + vectors,
        check_vma=False,
    )
```

```python
import functools

import jax
import jax.numpy as jnp
from jax import lax
from jax.experimental import pallas as pl
from jax.experimental.pallas import tpu as pltpu
from jax.sharding import PartitionSpec as P

HEADS = 12
HEAD_DIM = 64
EPSILON = 1e-12
NEGATIVE = -1000000000.0
DOCS = 4
LONGEST = 512
BIG = float(2**30)
PIECES = 8
WIDTH = ("y", "core")
DP = ("z", "x")
WIDTHS = 4
bf16 = jnp.bfloat16
f32 = jnp.float32
MIB = 2**20
NN = (((1,), (0,)), ((), ()))
NT = (((1,), (1,)), ((), ()))
TN = (((0,), (0,)), ((), ()))
SMEM = pl.BlockSpec(memory_space=pltpu.SMEM)
ANY = pl.BlockSpec(memory_space=pl.ANY)


def dot(a, b, dims=NN):
    return lax.dot_general(a, b, dims, preferred_element_type=f32)


def params(mib):
    return pltpu.CompilerParams(vmem_limit_bytes=mib * MIB)


SHORT = pl.CostEstimate(flops=1, bytes_accessed=1, transcendentals=0)


def ignoring(kernel, at, count):
    return lambda *refs: kernel(*refs[:at], *refs[at + count :])


def whole(shape):
    return pl.BlockSpec(shape, lambda *_: (0,) * len(shape))


def shape_of(shape, kind=bf16):
    return jax.ShapeDtypeStruct(shape, kind)


def slot_of(piece, home):
    return ((piece & 1) ^ (home & 1)) * 4 + ((piece >> 1) ^ (home >> 1))


def mix_kernel(src_ref, x_ref, mixed_ref):
    rows, total = src_ref.shape[0], x_ref.shape[0]
    pick = src_ref[...] == lax.broadcasted_iota(jnp.int32, (rows, total), 1)
    mixed_ref[...] = dot(jnp.where(pick, 1.0, 0.0).astype(bf16), x_ref[...]).astype(bf16)


def mix(src_col, x):
    total, width = x.shape
    return pl.pallas_call(
        mix_kernel,
        in_specs=[whole((total, 1)), whole((total, width))],
        out_specs=whole((total, width)),
        out_shape=shape_of((total, width)),
        compiler_params=params(14),
        cost_estimate=SHORT,
        name="mix",
    )(src_col, x)


def pack_kernel(sc, wq, wv, near_ref):
    half, part = wq.shape[0] // 2, wq.shape[1] // 2
    rows = pl.ds(pl.multiple_of((sc[0] >> 1) * half, 16), half)
    lanes = pl.ds(pl.multiple_of((sc[0] & 1) * part, 128), part)
    near_ref[:half, :] = wv[rows, lanes]
    near_ref[half:, :] = wq[rows, lanes]


def pack(sc, wq, wv, dep):
    rows, width = wq.shape
    shape = rows, width // 2
    return pl.pallas_call(
        ignoring(pack_kernel, 3, 1),
        in_specs=[SMEM, whole(wq.shape), whole(wv.shape), ANY],
        out_specs=whole(shape),
        out_shape=shape_of(shape),
        compiler_params=params(8),
        cost_estimate=SHORT,
        name="pack",
    )(sc, wq, wv, dep)


def pack_key_kernel(sc, wk, *refs):
    vectors, key_ref = refs[:9], refs[-1]
    rows, part = wk.shape[0], wk.shape[1] // 2
    line = jnp.concatenate([ref[...].astype(f32) for ref in vectors], axis=1)
    lines = [line[:, i * part : (i + 1) * part] for i in range(3)] + [jnp.zeros((13, part), f32)]
    key_ref[:rows, :] = wk[:, pl.ds(pl.multiple_of((sc[0] & 1) * part, 128), part)]
    key_ref[rows:, :] = jnp.concatenate(lines, axis=0).astype(bf16)


def pack_key(sc, wk, vectors, dep):
    rows, width = wk.shape
    lines = [v[None] for v in vectors]
    shape = rows + 16, width // 2
    return pl.pallas_call(
        ignoring(pack_key_kernel, 2 + len(lines), 1),
        in_specs=[SMEM] + [whole(a.shape) for a in (wk, *lines)] + [ANY],
        out_specs=whole(shape),
        out_shape=shape_of(shape),
        compiler_params=params(8),
        cost_estimate=SHORT,
        name="pack_key",
    )(sc, wk, *lines, dep)


def pack_rest_kernel(sc, wi, wo, wu, rest_ref):
    rows, width = wo.shape
    core = sc[0] & 1
    for quarter in range(2):
        at = pl.multiple_of((2 * core + quarter) * width, 128)
        rest_ref[quarter * rows : (quarter + 1) * rows, :] = wi[:, pl.ds(at, width)]
    rest_ref[2 * rows : 4 * rows, :] = wu[pl.ds(pl.multiple_of(core * 2 * rows, 16), 2 * rows), :]
    rest_ref[4 * rows :, :] = wo[pl.ds(pl.multiple_of(core * (rows // 2), 16), rows // 2), :]


def pack_rest(sc, wi, wo, wu):
    rows, width = wo.shape
    shape = rows * 9 // 2, width
    return pl.pallas_call(
        pack_rest_kernel,
        in_specs=[SMEM, whole(wi.shape), whole(wo.shape), whole(wu.shape)],
        out_specs=whole(shape),
        out_shape=shape_of(shape),
        compiler_params=params(8),
        cost_estimate=SHORT,
        name="pack_rest",
    )(sc, wi, wo, wu)


def fetch_parts(sc, sources, base, weight, sem):
    rows, part = weight.shape[0] // PIECES, weight.shape[1] // 2
    step = rows // 2
    for slot, source in enumerate(sources):
        where = sc[0] ^ slot
        at = pl.multiple_of((where & 1) * part, 128)
        for piece in range(PIECES):
            to = pl.multiple_of(piece * rows + (where >> 1) * step, 16)
            pltpu.make_async_copy(
                source.at[slot_of(piece, sc[1]), pl.ds(base, step), :],
                weight.at[pl.ds(to, step), pl.ds(at, part)],
                sem,
            ).start()


def fetch_halves(sc, sources, weight, sem):
    rows, part = weight.shape[0] // PIECES, weight.shape[1] // 2
    for other, source in enumerate(sources):
        at = pl.multiple_of(((sc[0] & 1) ^ other) * part, 128)
        for piece in range(PIECES):
            pltpu.make_async_copy(
                source.at[slot_of(piece, sc[1]), pl.ds(0, rows), :],
                weight.at[pl.ds(piece * rows, rows), pl.ds(at, part)],
                sem,
            ).start()


def project_kernel(fetch, scale, sc, mixed_ref, bias_ref, *refs):
    parts, outs, (weight, sem) = refs[:-5], refs[-5:-2], refs[-2:]
    fetch(sc, parts, weight, sem)
    pltpu.make_async_copy(weight, weight, sem).wait()
    for start in range(0, mixed_ref.shape[0], 512):
        rows = pl.ds(start, 512)
        out = dot(mixed_ref[rows, :], weight[...]) + bias_ref[...].astype(f32)
        out = out.astype(bf16) * jnp.asarray(scale, bf16)
        for third, ref in enumerate(outs):
            size = ref.shape[1]
            ref[rows, :] = out[:, third * size : (third + 1) * size]


def project(base, scale, sc, mixed, bias, parts):
    total, width = mixed.shape
    fetch = fetch_halves if base is None else lambda sc, parts, weight, sem: fetch_parts(sc, parts, base, weight, sem)
    return pl.pallas_call(
        functools.partial(project_kernel, fetch, scale),
        in_specs=[SMEM, whole((total, width)), whole((1, width))] + [ANY] * len(parts),
        out_specs=[whole((total, width // 3))] * 3 + [whole((width, width))],
        out_shape=[shape_of((total, width // 3))] * 3 + [shape_of((width, width))],
        scratch_shapes=[pltpu.SemaphoreType.DMA],
        compiler_params=params(10),
        cost_estimate=SHORT,
        name="project",
    )(sc, mixed, bias, *parts)


def doc_table(segments):
    number = jnp.arange(DOCS)[:, None]
    return jnp.stack([
        jnp.sum((segments[None, :] < number).astype(jnp.int32), axis=1),
        jnp.sum((segments[None, :] == number).astype(jnp.int32), axis=1),
    ])


def head_rows(value):
    lane = lax.broadcasted_iota(jnp.int32, value.shape, 1)
    none = jnp.zeros_like(value)
    return jnp.concatenate(
        [jnp.where(lane < HEAD_DIM, value, none), jnp.where(lane < HEAD_DIM, none, value)], axis=0
    )


def over_docs(docs, sizes, run):
    @pl.loop(0, DOCS)
    def _(doc):
        start, length = docs[0, doc], docs[1, doc]
        low = 0
        for size in sizes:

            @pl.when((length > low) & (length <= size))
            def _():
                run(start, length, size)

            low = size


def mask_columns(length, queries, keys):
    lane = lax.broadcasted_iota(jnp.int32, (keys, 128), 1)
    row = lax.broadcasted_iota(jnp.int32, (keys, 128), 0)
    of_keys = jnp.where((lane == 0) & (row >= length), 1.0, 0.0).astype(bf16)
    lane = lax.broadcasted_iota(jnp.int32, (queries, 128), 1)
    return jnp.where(lane == 0, -BIG, 0.0).astype(bf16), of_keys


def unpack(pairs, total, moves):
    for pair in range(pairs):
        for source, to in moves:
            to[pair, :total, :] = source[:, 128 * pair : 128 * (pair + 1)].astype(f32)
            to[pair, total:, :] = jnp.zeros((LONGEST, 128), f32)


def attend_kernel(first, pairs, sc, docs, q_ref, k_ref, v_ref, ctx_ref, wide_ref, lse_ref, qs, ks, vs, cs, ls):
    total = q_ref.shape[0]
    left = sc[3] - 2 * first
    step = 256

    @pl.when(left <= 0)
    def _():
        for ref in (ctx_ref, wide_ref, lse_ref):
            ref[...] = jnp.zeros_like(ref)

    @pl.when(left > 0)
    def _():
        unpack(pairs, total, ((q_ref, qs), (k_ref, ks), (v_ref, vs)))
        lane = lax.broadcasted_iota(jnp.int32, (step, 128), 1)

        def run(start, length, size):
            @pl.loop(0, (length + step - 1) // step)
            def _(block):
                rows, keys = pl.ds(start + block * step, step), pl.ds(start, size)
                of_queries, of_keys = mask_columns(length, 2 * step, size)
                stat = jnp.zeros((step, 128), f32)
                for pair in range(pairs):
                    queries = jnp.concatenate([head_rows(qs[pair, rows, :].astype(bf16)), of_queries], axis=1)
                    s = dot(queries, jnp.concatenate([ks[pair, keys, :].astype(bf16), of_keys], axis=1), NT)
                    top = jnp.max(s, axis=1, keepdims=True)
                    e = jnp.exp(s - top).astype(bf16)
                    values = jnp.concatenate([vs[pair, keys, :].astype(bf16), jnp.ones((size, 128), bf16)], axis=1)
                    out = dot(e, values)
                    norm = out[:, 128:129]
                    out = out[:, :128] * (1.0 / norm)
                    cs[pair, rows, :] = jnp.where(lane < HEAD_DIM, out[:step], out[step:])
                    logsum = top + jnp.log(norm)
                    stat = jnp.where(
                        lane == 2 * pair, logsum[:step], jnp.where(lane == 2 * pair + 1, logsum[step:], stat)
                    )
                ls[rows, :] = stat

        over_docs(docs, (256, 512), run)
        lane = lax.broadcasted_iota(jnp.int32, (total, 128), 1)
        for pair in range(pairs):
            lanes = slice(128 * pair, 128 * (pair + 1))
            value = jnp.where(lane < (left - 2 * pair) * HEAD_DIM, cs[pair, :total, :], 0.0)
            wide_ref[:, lanes] = value
            ctx_ref[:, lanes] = value.astype(bf16)
        lse_ref[...] = ls[:total, :]


def attend(third, sc, docs, q, k, v, deps=()):
    total, width = q.shape
    pairs = width // 128
    cols = out = whole((total, width))
    return pl.pallas_call(
        ignoring(functools.partial(attend_kernel, pairs * third, pairs), 5, len(deps)),
        in_specs=[SMEM, SMEM, cols, cols, cols] + [ANY] * len(deps),
        out_specs=[out, out, whole((total, 128))],
        out_shape=[shape_of((total, width)), shape_of((total, width), f32), shape_of((total, 128), f32)],
        scratch_shapes=[pltpu.VMEM((pairs, total + LONGEST, 128), f32)] * 4 + [pltpu.VMEM((total + LONGEST, 128), f32)],
        compiler_params=params(16),
        cost_estimate=SHORT,
        name="attend",
    )(sc, docs, q, k, v, *deps)


def attend_back_kernel(
    first, pairs, sc, docs, q_ref, k_ref, v_ref, c_ref, wide_ref, lse_ref,
    dq_ref, dk_ref, dv_ref, sums_ref, qs, ks, vs, cs, xs, ls,
):
    total = q_ref.shape[0]
    left = sc[3] - 2 * first

    @pl.when(left <= 0)
    def _():
        for ref in (dq_ref, dk_ref, dv_ref, sums_ref):
            ref[...] = jnp.zeros_like(ref)

    @pl.when(left > 0)
    def _():
        unpack(pairs, total, ((q_ref, qs), (k_ref, ks), (v_ref, vs), (c_ref, cs), (wide_ref, xs)))
        ls[:total, :] = lse_ref[...]
        ls[total:, :] = jnp.zeros((LONGEST, 128), f32)

        def run(start, length, size):
            rows = pl.ds(start, size)
            lane = lax.broadcasted_iota(jnp.int32, (size, 128), 1)
            live = lax.broadcasted_iota(jnp.int32, (size, 128), 0) < length
            of_queries, of_keys = mask_columns(length, 2 * size, size)
            logsums = jnp.where(live, ls[rows, :], BIG)
            for pair in range(pairs):
                queries = head_rows(qs[pair, rows, :].astype(bf16))
                grad = jnp.where(live, cs[pair, rows, :], 0.0)
                grads = head_rows(grad.astype(bf16))
                inner = grad * xs[pair, rows, :]
                delta = jnp.concatenate([
                    jnp.sum(jnp.where(lane < HEAD_DIM, inner, 0.0), axis=1, keepdims=True),
                    jnp.sum(jnp.where(lane < HEAD_DIM, 0.0, inner), axis=1, keepdims=True),
                ], axis=0)
                logsum = jnp.concatenate(
                    [logsums[:, 2 * pair : 2 * pair + 1], logsums[:, 2 * pair + 1 : 2 * pair + 2]], axis=0
                )
                keys = ks[pair, rows, :].astype(bf16)
                s = dot(jnp.concatenate([queries, of_queries], axis=1), jnp.concatenate([keys, of_keys], axis=1), NT)
                dp = dot(grads, vs[pair, rows, :].astype(bf16), NT)
                p = jnp.exp(s - logsum)
                ds = (p * (dp - delta)).astype(bf16)
                dv = dot(p.astype(bf16), grads, TN)
                dk = dot(ds, queries, TN)
                dq = dot(ds, keys)
                dq = jnp.where(lane < HEAD_DIM, dq[:size], dq[size:]) * HEAD_DIM**-0.5
                qs[pair, rows, :] = jnp.where(live, dq, qs[pair, rows, :])
                ks[pair, rows, :] = jnp.where(live, dk, ks[pair, rows, :])
                vs[pair, rows, :] = jnp.where(live, dv, vs[pair, rows, :])

        over_docs(docs, (128, 256, 384, 512), run)
        for pair in range(pairs):
            lanes = slice(128 * pair, 128 * (pair + 1))
            for to, value in ((dq_ref, qs), (dk_ref, ks), (dv_ref, vs)):
                to[:, lanes] = value[pair, :total, :].astype(bf16)
        sums_ref[0:1, :] = col_sum(dq_ref[...].astype(f32))
        sums_ref[1:2, :] = col_sum(dv_ref[...].astype(f32))


def attend_back(third, sc, docs, q, k, v, c, wide, lse, deps=()):
    total, width = q.shape
    pairs = width // 128
    cols = out = whole((total, width))
    return pl.pallas_call(
        ignoring(functools.partial(attend_back_kernel, pairs * third, pairs), 8, len(deps)),
        in_specs=[SMEM, SMEM, cols, cols, cols, cols, out, whole((total, 128))] + [ANY] * len(deps),
        out_specs=[out] * 3 + [whole((8, width))],
        out_shape=[shape_of((total, width))] * 3 + [shape_of((8, width), f32)],
        scratch_shapes=[pltpu.VMEM((pairs, total + LONGEST, 128), f32)] * 5 + [pltpu.VMEM((total + LONGEST, 128), f32)],
        compiler_params=params(22),
        cost_estimate=SHORT,
        name="attend_back",
    )(sc, docs, q, k, v, c, wide, lse, *deps)


def row_mean(value):
    return jnp.mean(value, axis=1, keepdims=True)


def normalise(hidden):
    centred = hidden - row_mean(hidden)
    rate = lax.rsqrt(row_mean(centred * centred) + EPSILON)
    return centred * rate, rate


def norm_back(grad, gain, unit, rate):
    scaled = grad * gain
    return rate * (scaled - row_mean(scaled) - unit * row_mean(scaled * unit))


def col_sum(value):
    return jnp.sum(value, axis=0, keepdims=True)


def feed_kernel(
    sc, mixed_ref, c0, c1, c2, cot_hbm, bi_ref, vec_ref, *refs
):
    rest = refs[0]
    (out_hbm, d0, d1, d2, flow_ref, dbi_ref, sums_ref, keep_i, send_i, keep_u, send_u,
     wi, wu, wo, act, slope, unit_ref, grad_ref, low_ref, glow_ref, rate_ref, cot_ref, stage, first_ref,
     wo_sem, wi_sem, wu_sem, stage_sem, cot_sem, out_sem) = refs[1:]
    total, width = mixed_ref.shape
    unit_rows = width // PIECES
    outer_rows = WIDTHS * width // PIECES
    own, home, active, heads = sc[0], sc[1], sc[2], sc[3]
    ob, g1, s1, ub, g2, s2 = (vec_ref[i : i + 1, :].astype(f32) for i in range(6))

    for half in range(2):
        pltpu.make_async_copy(
            rest.at[half, :, pl.ds(4 * unit_rows, unit_rows // 2), :], wo.at[:, half], wo_sem.at[half]
        ).start()
    for slot in range(WIDTHS):
        quarter = own ^ slot
        at = pl.multiple_of((quarter & 1) * unit_rows, 16)
        pltpu.make_async_copy(
            rest.at[quarter >> 1, :, pl.ds(at, unit_rows), :], wi.at[slot], wi_sem.at[slot]
        ).start()
        for half in range(2):
            pltpu.make_async_copy(
                rest.at[half, pl.ds(2 * quarter, 2), pl.ds(2 * unit_rows, 2 * unit_rows), :],
                wu.at[slot, :, half],
                wu_sem.at[slot, half],
            ).start()
    cot_copy = pltpu.make_async_copy(cot_hbm, cot_ref, cot_sem)
    cot_copy.start()

    def inner_weight(slot):
        return wi[slot].reshape(width, width)

    def outer(slot):
        return wu[slot].reshape(width, width)

    def output():
        return wo[...].reshape(width, width)

    step = 256
    blocks = [pl.ds(i * step, step) for i in range(total // step)]
    for half in range(2):
        pltpu.make_async_copy(wo.at[:, half], wo.at[:, half], wo_sem.at[half]).wait()
    for rows in blocks:
        ctx = jnp.concatenate([c0[rows, :], c1[rows, :], c2[rows, :]], axis=1)
        unit, rate = normalise(mixed_ref[rows, :].astype(f32) + dot(ctx, output()) + ob)
        unit_ref[rows, :] = unit
        rate_ref[rows, :] = rate
        normed = unit * g1 + s1
        low_ref[rows, :] = normed.astype(bf16)
        first_ref[rows, :] = normed + ub
    for slot in range(WIDTHS):
        quarter = own ^ slot
        pltpu.make_async_copy(wi.at[slot], wi.at[slot], wi_sem.at[slot]).wait()
        for half in range(2):
            pltpu.make_async_copy(wu.at[slot, :, half], wu.at[slot, :, half], wu_sem.at[slot, half]).wait()

        @pl.when(quarter < active)
        def _():
            bias = bi_ref[quarter].astype(f32)
            for rows in blocks:
                inner = dot(low_ref[rows, :], inner_weight(slot)) + bias
                phi = 0.5 * (1.0 + lax.erf(inner * 0.7071067811865476))
                act[slot, rows, :] = (inner * phi).astype(bf16)
                density = jnp.exp(-0.5 * inner * inner) * 0.3989422804014327
                slope[slot, rows, :] = (phi + inner * density).astype(bf16)
            first_ref[...] += dot(act[slot], outer(slot))

    sums_ref[...] = jnp.zeros_like(sums_ref)
    cot_copy.wait()
    for rows in blocks:
        unit, rate = normalise(first_ref[rows, :])
        cot = cot_ref[rows, :].astype(f32)
        cot_ref[rows, :] = (unit * g2 + s2).astype(bf16)
        grad = norm_back(cot, g2, unit, rate)
        grad_ref[rows, :] = grad
        low = grad.astype(bf16)
        glow_ref[rows, :] = low
        sums_ref[3:4, :] += col_sum(low.astype(f32))
        sums_ref[4:5, :] += col_sum(cot * unit)
        sums_ref[5:6, :] += col_sum(cot)
    out_copy = pltpu.make_async_copy(cot_ref, out_hbm, out_sem)
    out_copy.start()
    first_ref[...] = grad_ref[...]

    def staged(slot):
        for i in range(2):
            pltpu.make_async_copy(stage.at[slot & 1, i], stage.at[slot & 1, i], stage_sem.at[slot & 1, i]).wait()

    for slot in range(WIDTHS):
        quarter = own ^ slot
        here = slot & 1

        if slot > 1:
            staged(slot)

        @pl.when(quarter >= active)
        def _():
            stage[here] = jnp.zeros((2, width, width), bf16)
            dbi_ref[quarter] = jnp.zeros((1, width), f32)

        @pl.when(quarter < active)
        def _():
            stage[here, 1] = dot(act[slot], glow_ref[...], TN).astype(bf16)
            inner = (dot(glow_ref[...], outer(slot), NT) * slope[slot].astype(f32)).astype(bf16)
            dbi_ref[quarter] = col_sum(inner.astype(f32))
            stage[here, 0] = dot(low_ref[...], inner, TN).astype(bf16)
            first_ref[...] += dot(inner, inner_weight(slot), NT)

        to = (keep_i, send_i)[slot & 1]
        for piece in range(PIECES):
            pltpu.make_async_copy(
                stage.at[here, 0, pl.ds(piece * unit_rows, unit_rows), :],
                to.at[slot >> 1, slot_of(piece, home)],
                stage_sem.at[here, 0],
            ).start()
        for end in range(2):
            for part in range(WIDTHS):
                at = pl.multiple_of(end * outer_rows + (own ^ part) * unit_rows, 16)
                pltpu.make_async_copy(
                    stage.at[here, 1, pl.ds(at, unit_rows), :],
                    (keep_u, send_u)[part & 1].at[part >> 1, slot_of(2 * quarter + end, home)],
                    stage_sem.at[here, 1],
                ).start()

    for rows in blocks:
        unit = unit_ref[rows, :]
        normed_grad = first_ref[rows, :]
        first = norm_back(normed_grad, g1, unit, rate_ref[rows, :])
        low = first.astype(bf16)
        flow_ref[rows, :] = low
        dctx = dot(low, output(), NT)
        lane = lax.broadcasted_iota(jnp.int32, dctx.shape, 1)
        dctx = jnp.where(lane < heads * HEAD_DIM, dctx, 0.0).astype(bf16)
        for third, ref in enumerate((d0, d1, d2)):
            size = ref.shape[1]
            ref[rows, :] = dctx[:, third * size : (third + 1) * size]
        sums_ref[0:1, :] += col_sum(low.astype(f32))
        sums_ref[1:2, :] += col_sum(normed_grad * unit)
        sums_ref[2:3, :] += col_sum(normed_grad)
    staged(WIDTHS - 2)
    staged(WIDTHS - 1)
    out_copy.wait()


def feed(sc, mixed, contexts, cot, bi, vec, rest):
    total, width = mixed.shape
    square = whole((total, width))
    piece = (2, PIECES, width // PIECES, width)
    return pl.pallas_call(
        feed_kernel,
        in_specs=[SMEM, square] + [whole((total, width // 3))] * 3 + [ANY, whole(bi.shape), whole(vec.shape)]
        + [ANY],
        out_specs=[ANY] + [whole((total, width // 3))] * 3 + [square, whole((WIDTHS, 1, width)), whole((8, width))]
        + [ANY] * 4,
        out_shape=[
            shape_of((total, width)), *[shape_of((total, width // 3))] * 3,
            shape_of((total, width)), shape_of((WIDTHS, 1, width), f32), shape_of((8, width), f32),
        ] + [shape_of(piece)] * 4,
        scratch_shapes=[
            pltpu.VMEM((WIDTHS, PIECES, width // PIECES, width), bf16),
            pltpu.VMEM((WIDTHS, 2, 2, width // 4, width), bf16),
            pltpu.VMEM((PIECES, 2, width // PIECES // 2, width), bf16),
            pltpu.VMEM((WIDTHS, total, width), bf16), pltpu.VMEM((WIDTHS, total, width), bf16),
            pltpu.VMEM((total, width), f32), pltpu.VMEM((total, width), f32),
            pltpu.VMEM((total, width), bf16), pltpu.VMEM((total, width), bf16), pltpu.VMEM((total, 1), f32),
            pltpu.VMEM((total, width), bf16), pltpu.VMEM((2, 2, width, width), bf16), pltpu.VMEM((total, width), f32),
            pltpu.SemaphoreType.DMA((2,)), pltpu.SemaphoreType.DMA((WIDTHS,)), pltpu.SemaphoreType.DMA((WIDTHS, 2)),
            pltpu.SemaphoreType.DMA((2, 2)), pltpu.SemaphoreType.DMA, pltpu.SemaphoreType.DMA,
        ],
        compiler_params=params(60),
        cost_estimate=SHORT,
        name="feed",
    )(sc, mixed, *contexts, cot, bi, vec, rest)


def project_grad_kernel(thirds, with_lines, sc, mixed_ref, ctx0, ctx1, ctx2, low_ref, *refs):
    grads, lines = refs[: 3 * len(thirds)], refs[3 * len(thirds)] if with_lines else None
    keep, send = refs[-2:]
    total, width = mixed_ref.shape
    part = width // 3
    rows = width // PIECES
    own, home = sc[0], sc[1]
    for matrix in range(4):
        if matrix < 3:
            left = mixed_ref[...]
            right = jnp.concatenate([grads[3 * i + matrix][...] for i in range(len(thirds))], axis=1)
        else:
            left = jnp.concatenate([ctx0[...], ctx1[...], ctx2[...]], axis=1)
            right = low_ref[:, thirds[0] * part : (thirds[-1] + 1) * part]
        value = dot(left, right, TN).astype(bf16)
        slot = matrix ^ own

        def put(ref):
            for piece in range(PIECES):
                side, to = slot >> 1, slot_of(piece, home)
                ref[side, to, pl.ds(0, rows), :] = value[piece * rows : (piece + 1) * rows]
                if with_lines:
                    ref[side, to, pl.ds(rows, 16), :] = lines[piece, matrix]

        @pl.when((slot & 1) == 0)
        def _():
            put(keep)

        @pl.when((slot & 1) == 1)
        def _():
            put(send)


def project_grad(thirds, sc, mixed, contexts, low, grads, lines=None, deps=()):
    total, width = mixed.shape
    part = width // 3
    extra = [] if lines is None else [lines]
    flat = [a for group in grads for a in group]
    pack = (2, PIECES, width // PIECES + 16 * len(extra), part * len(thirds))
    count = 6 + len(flat) + len(extra)
    return pl.pallas_call(
        ignoring(functools.partial(project_grad_kernel, thirds, bool(extra)), count, len(deps)),
        in_specs=[SMEM, whole((total, width))] + [whole((total, part))] * 3 + [whole((total, width))]
        + [whole((total, part))] * len(flat) + [whole(a.shape) for a in extra] + [ANY] * len(deps),
        out_specs=[whole(pack), whole(pack)],
        out_shape=[shape_of(pack), shape_of(pack)],
        compiler_params=params(16),
        cost_estimate=SHORT,
        name="project_grad",
    )(sc, mixed, *contexts, low, *flat, *extra, *deps)


def input_grad_kernel(src_row, first_ref, wq, wk, wv, *refs):
    grads, out_ref, joined, low_ref = refs[:-3], *refs[-3:]
    total, width = first_ref.shape
    block = pl.program_id(0)
    rows = out_ref.shape[0]

    @pl.when(block == 0)
    def _():
        part = width // 3
        for third in range(3):
            for i in range(3):
                joined[i, :, third * part : (third + 1) * part] = grads[3 * third + i][...]
        grad = first_ref[...].astype(f32)
        for i, weight in enumerate((wq, wk, wv)):
            grad = grad + dot(joined[i], weight[...], NT)
        low_ref[...] = grad.astype(bf16)

    target = lax.broadcasted_iota(jnp.int32, (rows, total), 0) + block * rows
    place = jnp.where(target == src_row[...], 1.0, 0.0).astype(bf16)
    out_ref[...] = dot(place, low_ref[...])


def input_grad(src_row, first, weights, grads, deps=(), tile=512):
    total, width = first.shape
    flat = [a for group in grads for a in group]
    return pl.pallas_call(
        ignoring(input_grad_kernel, 5 + len(flat), len(deps)),
        grid=(total // tile,),
        in_specs=[whole(src_row.shape), whole((total, width))] + [whole((width, width))] * 3
        + [whole((total, width // 3))] * len(flat) + [ANY] * len(deps),
        out_specs=pl.BlockSpec((tile, width), lambda i: (i, 0)),
        out_shape=shape_of((total, width), f32),
        scratch_shapes=[pltpu.VMEM((3, total, width), bf16), pltpu.VMEM((total, width), bf16)],
        compiler_params=params(26),
        cost_estimate=SHORT,
        name="input_grad",
    )(src_row, first, *weights, *flat, *deps)


def finish_feed_kernel(sc, f0, f1, f2, f3, gi, gu):
    rows, width = gi.shape[0], gu.shape[1]
    for slot, ref in enumerate((f0, f1, f2, f3)):
        quarter = sc[0] ^ slot
        gi[:, pl.ds(pl.multiple_of(quarter * width, 128), width)] = ref[0].astype(f32)
        gu[pl.ds(pl.multiple_of(quarter * rows, 8), rows), :] = ref[1].astype(f32)


def finish_feed(sc, parts, rows, width):
    shapes = [(rows, WIDTHS * width), (WIDTHS * rows, width)]
    return pl.pallas_call(
        finish_feed_kernel,
        in_specs=[SMEM] + [whole(a.shape) for a in parts],
        out_specs=[whole(s) for s in shapes],
        out_shape=[shape_of(s, f32) for s in shapes],
        compiler_params=params(8),
        cost_estimate=SHORT,
        name="finish_feed",
    )(sc, *parts)


def finish_kernel(cut, sc, *refs):
    parts, matrices, vectors = refs[:4], refs[4:8], refs[8:]
    rows, width = matrices[0].shape
    size = rows * 12 // 4
    for own in range(WIDTHS):

        @pl.when(sc[0] == own)
        def _():
            line = []
            for matrix, ref in enumerate(matrices):
                part = parts[matrix ^ own]
                ref[...] = part[:rows, :].astype(f32)
                tail = part[rows : rows + 16, cut:].astype(f32)
                line += [tail[0:1], tail[1:2, : size - (width - cut)]]
            line = jnp.concatenate(line, axis=1)
            at = 0
            for ref in vectors:
                ref[...] = line[:, at : at + ref.shape[1]]
                at += ref.shape[1]


def finish(sc, parts, rows, width, cut):
    sizes = [rows] * 8 + [WIDTHS * rows]
    shapes = [(rows, width)] * 4 + [(1, n) for n in sizes]
    return pl.pallas_call(
        functools.partial(finish_kernel, cut),
        in_specs=[SMEM] + [whole(a.shape) for a in parts],
        out_specs=[whole(s) for s in shapes],
        out_shape=[shape_of(s, f32) for s in shapes],
        compiler_params=params(8),
        cost_estimate=SHORT,
        name="finish",
    )(sc, *parts)


def exchange(value, axis, bits=1):
    size = lax.axis_size(axis)
    return lax.ppermute(value, axis, [(i, i ^ bits) for i in range(size)])


def join_kernel(count, *refs):
    out = refs[-1]
    at = 0
    for ref in refs[:count]:
        size = ref.shape[0]
        out[at : at + size] = ref[...]
        at += size


def join(parts, deps=()):
    shape = (sum(a.shape[0] for a in parts), *parts[0].shape[1:])
    return pl.pallas_call(
        functools.partial(join_kernel, len(parts)),
        in_specs=[whole(a.shape) for a in parts] + [ANY] * len(deps),
        out_specs=whole(shape),
        out_shape=shape_of(shape),
        compiler_params=params(8),
        cost_estimate=SHORT,
        name="join",
    )(*parts, *deps)


def along_z(piece):
    piece = piece[None]
    return [piece] + [exchange(piece, "z", k) for k in (1, 2, 3)]


def add(*terms):
    total = terms[0].astype(f32)
    for term in terms[1:]:
        total = total + term.astype(f32)
    return total.astype(bf16)


def sums_kernel(plan, count, *refs):
    inputs, outputs = refs[:count], refs[-len(plan) :]
    for blocks, out in zip(plan, outputs):
        for at, terms in blocks:
            total = 0.0
            for index, where in terms:
                total = total + inputs[index][where].astype(f32)
            out[at] = total.astype(bf16)


def sums(plan, shapes, inputs, deps=()):
    return pl.pallas_call(
        functools.partial(sums_kernel, plan, len(inputs)),
        in_specs=[whole(a.shape) for a in inputs] + [ANY] * len(deps),
        out_specs=[whole(shape) for shape in shapes],
        out_shape=[shape_of(shape) for shape in shapes],
        compiler_params=params(12),
        cost_estimate=SHORT,
        name="sums",
    )(*inputs, *deps)


def swap(keep, send):
    other = exchange(send, "core")
    return add(keep[0], other[0]), add(keep[1], other[1])


def spread(value):
    far = exchange(value, "y")
    return value, exchange(value, "core"), far, exchange(far, "core")


def per_device(
    inputs, cotangent, replacement_ids, augmented_count, segment_ids,
    query_weight, key_weight, value_weight, output_weight, inner_weight, outer_weight,
    query_bias, value_bias, output_bias, inner_bias, outer_bias,
    attention_gain, attention_shift, feed_gain, feed_shift,
):
    total, width = inputs.shape[1:]
    group = lax.axis_index(WIDTH)
    groups = lax.axis_size(WIDTH)
    shards = lax.axis_size(DP)
    direct = shards == PIECES and groups == WIDTHS
    rows = query_weight.shape[0]
    piece_rows = width // PIECES
    part = width // 2
    heads = HEADS * (group + 1) // groups
    own, home = (group, lax.axis_index(DP)) if direct else (jnp.zeros_like(group),) * 2
    sc = jnp.stack([own, home, group + 1, heads]).astype(jnp.int32)

    positions = jnp.arange(total, dtype=jnp.int32)
    sources = jnp.where(positions < augmented_count[0, 0], replacement_ids[0], positions)
    docs = doc_table(segment_ids[0, 0])
    mixed = mix(sources[:, None], inputs[0])

    vectors = (query_bias, value_bias, output_bias, attention_gain, attention_shift,
               outer_bias, feed_gain, feed_shift, inner_bias)
    if direct:
        rest = pack_rest(sc, inner_weight, output_weight, outer_weight)
        near_piece = pack(sc, query_weight, value_weight, rest)
        near_column = along_z(near_piece)
        rest = lax.all_gather(rest, ("core", *DP), axis=0, tiled=True).reshape(2, PIECES, -1, width)
        key_piece = pack_key(sc, key_weight, vectors, near_column[1])
        key_column = along_z(key_piece)
        near_column = join(near_column, [key_piece])
        near = join([near_column, exchange(near_column, "x")])
        near_parts = spread(near)
        key_column = join(key_column)
        key_near = join([key_column, exchange(key_column, "x")])
        key_parts = [key_near, exchange(key_near, "core")]
        order = jnp.stack([slot_of(p, home) for p in range(PIECES)])
        lines = jnp.take(key_near[:, rows : rows + 3, :].reshape(PIECES, 3 * part), order, axis=0)
        key_base, value_base, query_base = None, 0, rows // 2
        value_parts = query_parts = near_parts
    else:
        everything = lambda a: lax.all_gather(a, DP, axis=0, tiled=True)
        slots = [(s & 3) * 2 + (s >> 2) for s in range(PIECES)]
        by_piece = lambda a: jnp.stack([a.reshape(PIECES, -1, a.shape[-1])[p] for p in slots])
        step = piece_rows // 2
        plain = lambda a: a.reshape(PIECES, -1, a.shape[-1])
        full = [by_piece(everything(a)) for a in (key_weight, value_weight, query_weight)]
        key_parts, value_parts, query_parts = (
            [a[:, (s >> 1) * step : (s >> 1) * step + step, (s & 1) * part : (s & 1) * part + part] for s in range(4)]
            for a in full
        )
        key_base = value_base = query_base = 0
        inner_full = plain(everything(inner_weight))
        outer_rows, output_rows = plain(everything(outer_weight)), plain(everything(output_weight))
        rest = jnp.stack([
            jnp.concatenate([
                inner_full[:, :, 2 * h * width : (2 * h + 1) * width],
                inner_full[:, :, (2 * h + 1) * width : (2 * h + 2) * width],
                outer_rows[:, h * 2 * piece_rows : (h + 1) * 2 * piece_rows],
                output_rows[:, h * step : (h + 1) * step],
            ], 1)
            for h in range(2)
        ])
        lines = jnp.concatenate([everything(a).reshape(PIECES, -1) for a in vectors], 1)
    small = lines[:, :width].reshape(PIECES, 8, piece_rows).transpose(1, 0, 2).reshape(8, width)
    inner_bias_full = lines[:, width:].reshape(WIDTHS, 1, width)
    vec = small[2:]

    *keys, key_full = project(key_base, 1.0, sc, mixed, jnp.zeros((1, width), bf16), key_parts)
    *values, value_full = project(value_base, 1.0, sc, mixed, small[1:2], value_parts)
    *queries, query_full = project(query_base, HEAD_DIM**-0.5, sc, mixed, small[0:1], query_parts)
    qkv = [(queries[third], keys[third], values[third]) for third in range(3)]
    attended = [attend(0, sc, docs, *qkv[0])]
    for third in (1, 2):
        attended.append(attend(third, sc, docs, *qkv[third], [attended[-1][2]]))
    contexts = [a[0] for a in attended]
    out, *dctx, flow, dbi, norm_sums, keep_i, send_i, keep_u, send_u = feed(
        sc, mixed, contexts, cotangent[0], inner_bias_full, vec, rest
    )

    def back(third, *deps):
        _, wide, logsums = attended[third]
        *grads, bias = attend_back(
            third, sc, docs, queries[third], keys[third], values[third], dctx[third], wide, logsums, deps)
        return grads, bias

    def bias_lines(*biases):
        bias = jnp.concatenate([a[:2] for a in biases], axis=1)
        vector_grads = jnp.concatenate([bias, norm_sums[:6]])
        return jnp.concatenate(
            [vector_grads.reshape(8, PIECES, -1).transpose(1, 0, 2).reshape(PIECES, width), dbi.reshape(PIECES, -1)], 1)

    def padded(lines):
        lines = lines.astype(bf16).reshape(PIECES, WIDTHS, -1)
        lines = jnp.pad(lines, ((0, 0), (0, 0), (0, 2 * (width // 3) - lines.shape[2])))
        return jnp.pad(lines.reshape(PIECES, WIDTHS, 2, width // 3), ((0, 0), (0, 0), (0, 14), (0, 0)))

    weight_grads = functools.partial(project_grad, sc=sc, mixed=mixed, contexts=contexts, low=flow)
    if direct:
        near_u, far_u = swap(keep_u, send_u)
        near_i, far_i = swap(keep_i, send_i)
        grads0, bias0 = back(0, near_u, far_u, near_i, far_i)
        grads1, bias1 = back(1, bias0)
        keep_low, send_low = weight_grads((0, 1), grads=(grads0, grads1))
        over_u = exchange(jnp.concatenate([near_u[4:], far_u[4:]]), "x")
        over_i = exchange(far_i, "y")
        over_low = exchange(send_low, "core")
        front, back_half, all_of = slice(0, 4), slice(4, 8), slice(None)
        quad = (4, piece_rows, width)
        near_u, far_u, near_i, far_i = sums(
            [[(all_of, [(0, front), (2, front)])], [(all_of, [(1, front), (2, back_half)])],
             [(all_of, [(3, front), (4, front)])], [(all_of, [(3, back_half), (4, back_half)])]],
            [quad] * 4, [near_u, far_u, over_u, near_i, over_i], [keep_low])
        grads2, bias2 = back(2, near_u)
        lines = padded(bias_lines(bias0, bias1, bias2))
        over_u, over_i = exchange(far_u, "y"), exchange(far_i, "x")
        cols = keep_low.shape[3]
        octet = (PIECES, piece_rows, cols)
        column, near_low, far_low = sums(
            [[((all_of, 0), [(2, all_of), (3, all_of)]), ((all_of, 1), [(0, all_of), (1, all_of)])],
             [(all_of, [(4, 0), (5, 0)])], [(all_of, [(4, 1), (5, 1)])]],
            [(4, 2, piece_rows, width), octet, octet],
            [near_u, over_u, near_i, over_i, keep_low, over_low], [bias2])
        over_low = exchange(far_low, "y")
        columns = [column[:1]] + [exchange(column[k : k + 1], "z", k) for k in (1, 2, 3)]
        keep_high, send_high = weight_grads((2,), grads=(grads2,), lines=lines, deps=[column])
        tall, rest_cols = keep_high.shape[2:]
        octet = (PIECES, tall, rest_cols)
        near_high, far_high, sent = sums(
            [[(all_of, [(0, 0), (1, 0)])], [(all_of, [(0, 1), (1, 1)])],
             [(front, [(0, (0, back_half)), (1, (0, back_half))]), (back_half, [(0, (1, back_half)), (1, (1, back_half))])]],
            [octet] * 3, [keep_high, exchange(send_high, "core")])
        over_high = exchange(sent, "x")
        input_gradient = input_grad(
            sources[None, :], flow, (query_full, key_full, value_full), (grads0, grads1, grads2), [sent])
        feed_sum, = sums([[(all_of, [(k, 0) for k in range(4)])]], [(2, piece_rows, width)], columns, [input_gradient])
        feed_sums = spread(feed_sum)
        near_low, far_low, near_high, far_high = sums(
            [[(all_of, [(0, front), (1, front)])], [(all_of, [(0, back_half), (1, back_half)])],
             [(all_of, [(2, front), (4, front)])], [(all_of, [(3, front), (4, back_half)])]],
            [(4, piece_rows, cols)] * 2 + [(4, tall, rest_cols)] * 2,
            [near_low, over_low, near_high, far_high, over_high], [input_gradient, feed_sum])
        over_low, over_high = exchange(far_low, "x"), exchange(far_high, "y")
        left, right, top = slice(0, cols), slice(cols, width), slice(0, piece_rows)
        gi, gu = finish_feed(sc, feed_sums, rows, width)
        column, = sums(
            [[((all_of, top, left), [(0, all_of), (1, all_of)]), ((all_of, all_of, right), [(2, all_of), (3, all_of)])]],
            [(4, tall, width)], [near_low, over_low, near_high, over_high])
        columns = [column[:1]] + [exchange(column[k : k + 1], "z", k) for k in (1, 2, 3)]
        head_sum, = sums([[(all_of, [(k, 0) for k in range(4)])]], [(tall, width)], columns, [gi])
        head_sums = spread(head_sum)
        results = finish(sc, head_sums, rows, width, cols)
        gq, gk, gv, go = results[:4]
        bq, bv, bo, ga, sa, bu, gf, sf, bi = (a[0] for a in results[4:])
    else:
        grads, biases = zip(*[back(third) for third in range(3)])
        packs = weight_grads((0, 1), grads=grads[:2]), weight_grads((2,), grads=grads[2:])
        input_gradient = input_grad(sources[None, :], flow, (query_full, key_full, value_full), grads)
        ordered = [(p & 1) * 4 + (p >> 1) for p in range(PIECES)]
        in_order = lambda a: jnp.stack([a[s] for s in ordered])
        summed = lambda a: lax.psum(lax.psum_scatter(a, DP, scatter_dimension=0, tiled=True), WIDTH)
        total_sum = lambda a: summed(a.astype(f32))
        quarters_i = [keep_i[0], send_i[0], keep_i[1], send_i[1]]
        blocks_u = [keep_u[0], send_u[0], keep_u[1], send_u[1]]
        gi = total_sum(jnp.concatenate([in_order(a).reshape(width, width) for a in quarters_i], 1))
        gu = total_sum(jnp.stack([in_order(a) for a in blocks_u], 1).reshape(-1, width))
        gq, gk, gv, go = (
            total_sum(jnp.concatenate([in_order(packs[h][side][row]).reshape(width, -1) for h in range(2)], 1))
            for row, side in ((0, 0), (0, 1), (1, 0), (1, 1))
        )
        rows_of = bias_lines(*biases)
        vector_sums = rows_of[:, :width].reshape(PIECES, 8, piece_rows).transpose(1, 0, 2).reshape(8, width)
        bq, bv, bo, ga, sa, bu, gf, sf = (total_sum(a) for a in vector_sums)
        bi = total_sum(dbi.reshape(-1))
    return (out[None], input_gradient[None], gq, gk, gv, go, gi, gu, bq, bv, bo, bi, bu, ga, sa, gf, sf)


def solution(mesh):
    groups, shards = mesh.shape["width"], mesh.shape["dp"]
    fine = jax.sharding.Mesh(mesh.devices.reshape(groups // 2, 2, shards // 2, 2), (*WIDTH, *DP))
    tokens = (P(WIDTH, DP, None),) * 2 + (P(WIDTH, DP),) * 2 + (P(WIDTH, DP, None),)
    matrices = (P(DP, None),) * 6
    vectors = (P(DP),) * 9
    return jax.shard_map(
        per_device,
        mesh=fine,
        in_specs=tokens + matrices + vectors,
        out_specs=(P(WIDTH, DP, None),) * 2 + matrices + vectors,
        check_vma=False,
    )
```
